32 devices in a mesh: rep: 8 (over z, x), fsdp: 4 (over y, core).
Axes of the slice: x: 2, y: 2, z: 4, core: 2. Of those that a mesh axis runs over, the one named last changes fastest.
Arguments:
- hidden: bfloat16 [8, 1024, 4608], P('rep', 'fsdp'), may hold values from -6 to 6
- upstream: bfloat16 [8, 1024, 1024], P('rep', 'fsdp'), may hold values from -6 to 6
- weights: bfloat16 [8, 4608, 1024], P('rep', 'fsdp'), may hold values from -6 to 6
- moment_one: bfloat16 [8, 4608, 1024], P('rep', 'fsdp'), may hold values from -0.59765625 to 0.59765625
- moment_two: bfloat16 [8, 4608, 1024], P('rep', 'fsdp'), may hold values from 0.0029907227 to 0.099609375
- global_params: float32 [4, 1152, 1024], P('fsdp', 'rep'), may hold values from -6 to 6
- outer_momentum: float32 [4, 1152, 1024], P('fsdp', 'rep'), may hold values from -2 to 2
Outputs:
- values: bfloat16 [8, 1024, 1024], P('rep', 'fsdp')
- merged: bfloat16 [8, 4608, 1024], P('rep', 'fsdp')
- new_global: float32 [4, 1152, 1024], P('fsdp', 'rep')
- new_momentum: float32 [4, 1152, 1024], P('fsdp', 'rep')
The draws below stay inside these ranges and needn't reach their ends.
All inputs are finite; a program needn't handle non-finite values.
Results may differ from the reference program's by a relative error of at most 0.007.
Values may be sent and summed in bfloat16 or wider, within the bound.
A program may use at most 128 MiB of HBM per device.

```python
import math
import jax
import jax.numpy as jnp
from jax import lax

D = 4608
TOK_DEV = 256
COLS = 1024
RTOK = 1024
REPLICAS = 8
SHARDS = 4
FSDP_ROWS = 1152


def strengthened(result, own_key, source, target, blocks, factor):
    def block_of(axis_at):
        return (jnp.arange(result.shape[axis_at]) // (result.shape[axis_at] // blocks)).reshape((-1,) + (1,) * (result.ndim - 1 - axis_at))

    first = jax.random.permutation(own_key, blocks)[block_of(target)]
    second = (block_of(target) + blocks // 2) % blocks
    return jnp.where((block_of(source) == first) | (block_of(source) == second), factor * result, result)


def levels(stream_key, extent, shards, low, high):
    def one(dim, shards_of):
        steps = jax.random.uniform(jax.random.fold_in(jax.random.fold_in(stream_key, 6), dim), (shards_of,), jnp.float32, low / len(shards), high / len(shards))
        return jnp.repeat(jnp.exp(steps), extent[dim] // shards_of).reshape((-1,) + (1,) * (len(extent) - dim - 1))

    gain = one(*shards[0])
    for cut in shards[1:]:
        gain = gain * one(*cut)
    return gain


def noise(stream_key, dims, width, most, pieces=(), kind=jnp.bfloat16):
    result = jax.random.normal(stream_key, dims, jnp.float32) * width
    if len(pieces) > 0:
        result = levels(stream_key, dims, pieces, -0.22, 0.18) * result
    return jnp.clip(result, min=-most, max=most).astype(kind)


def noise_with(key, extent, width, bound, pieces, heavy, held_as=jnp.bfloat16):
    entries = width * jax.random.normal(key, extent, jnp.float32)
    if pieces:
        entries = entries * levels(key, extent, pieces, -0.22, 0.18)
    return jnp.clip(strengthened(entries, jax.random.fold_in(key, 3), *heavy), -bound, bound).astype(held_as)


def setup_inputs(seed: int = 0) -> dict:
    seeds = jax.random.split(jax.random.key(seed), 8)
    hidden = noise(seeds[0], (REPLICAS, RTOK, D), 1.0, 6.0, ((0, 8), (1, 4)))
    upstream = noise(seeds[1], (REPLICAS, RTOK, COLS), 1.0, 6.0, ((0, 8), (1, 4)))
    weights = noise_with(seeds[2], (REPLICAS, D, COLS), 1.0, 6.0, ((0, 8), (1, 4)), (0, 1, 8, 2.0))
    moment_one = noise(seeds[3], (REPLICAS, D, COLS), 0.1, 0.59765625, ((0, 8), (1, 4)))
    moment_two = jnp.clip(jnp.exp(math.log(0.099609375) - 3.5057412 * jax.random.uniform(seeds[4], (REPLICAS, D, COLS), jnp.float32) ** levels(seeds[4], (REPLICAS, D, COLS), ((0, 8), (1, 4)), -0.2, 0.2)), 0.0029907227, 0.099609375).astype(jnp.bfloat16)
    global_params = noise(seeds[5], (SHARDS, FSDP_ROWS, COLS), 1.0, 6.0, ((0, 4), (1, 8)), jnp.float32)
    outer_momentum = noise(seeds[6], (SHARDS, FSDP_ROWS, COLS), 0.3, 2.0, ((0, 4), (1, 8)), jnp.float32)
    return {"hidden": hidden, "upstream": upstream, "weights": weights, "moment_one": moment_one, "moment_two": moment_two, "global_params": global_params, "outer_momentum": outer_momentum}


beta_one = 0.9
beta_two = 0.95
bias_one = 1.0 - 0.9 ** 8
bias_two = 1.0 - 0.95 ** 8
inner_rate = 0.25
decay_rate = 0.1
epsilon = 1e-08
outer_rate = 0.7
outer_mu = 0.9
mixing = 0.5

def reference(hidden, upstream, weights, moment_one, moment_two, global_params, outer_momentum):
    factor = float(D) ** (-0.5)
    summed = lax.optimization_barrier(jnp.sum(weights, axis=0, dtype=jnp.float32))
    global_now = global_params.reshape(D, COLS)
    pseudo = global_now - summed / REPLICAS
    momentum = outer_mu * outer_momentum.reshape(D, COLS) + pseudo
    renewed = global_now - outer_rate * (pseudo + outer_mu * momentum)

    def per_replica(member):
        rows_in, grads_in, current_w, first_in, second_in = member
        outputs = (jnp.dot(rows_in, current_w, preferred_element_type=jnp.float32) * factor).astype(jnp.bfloat16)
        blocks_in = rows_in.reshape(SHARDS, TOK_DEV, D)
        blocks_grad = grads_in.reshape(SHARDS, TOK_DEV, COLS)
        gradient = jnp.zeros((D, COLS), jnp.float32)
        for position in range(SHARDS):
            partial_term = lax.dot_general(blocks_in[position], blocks_grad[position], (((0,), (0,)), ((), ())), preferred_element_type=jnp.float32) * factor
            rounded = lax.optimization_barrier(partial_term.astype(jnp.bfloat16))
            gradient = gradient + rounded.astype(jnp.float32)
        moment_new = beta_one * first_in.astype(jnp.float32) + (1.0 - beta_one) * gradient
        second_new = beta_two * second_in.astype(jnp.float32) + (1.0 - beta_two) * gradient * gradient
        stepped = moment_new / bias_one / (jnp.sqrt(second_new / bias_two) + epsilon)
        current = current_w.astype(jnp.float32)
        updated = current - inner_rate * (stepped + decay_rate * current)
        mixed = (mixing * updated + (1.0 - mixing) * renewed).astype(jnp.bfloat16)
        return (outputs, mixed)
    values, merged = lax.map(per_replica, (hidden, upstream, weights, moment_one, moment_two))
    return (values, merged, renewed.reshape(SHARDS, FSDP_ROWS, COLS), momentum.reshape(SHARDS, FSDP_ROWS, COLS))
```

```python
import functools

import jax
import jax.numpy as jnp
from jax import lax
from jax.experimental import pallas as pl
from jax.experimental.pallas import tpu as pltpu
from jax.sharding import PartitionSpec as P

beta_one = 0.9
beta_two = 0.95
bias_one = 1.0 - 0.9**8
bias_two = 1.0 - 0.95**8
inner_rate = 0.25
decay_rate = 0.1
epsilon = 1e-08
outer_rate = 0.7
outer_mu = 0.9
mixing = 0.5

MESH = pl.DeviceIdType.MESH
BF16 = jnp.bfloat16
F32 = jnp.float32
HALVES = 2
STRIP = 16


def inner_step(gradient, first, second, current):
    moment_new = beta_one * first + (1.0 - beta_one) * gradient
    second_new = beta_two * second + (1.0 - beta_two) * gradient * gradient
    stepped = moment_new / bias_one / (jnp.sqrt(second_new / bias_two) + epsilon)
    return current - inner_rate * (stepped + decay_rate * current)


def strips(rows, body):
    @pl.loop(0, rows // STRIP)
    def _(i):
        body(pl.multiple_of(i * STRIP, STRIP))


def fused(
    reps,
    hidden, upstream, weights, moment_one, moment_two, global_params, outer_momentum,
    values_out, merged_out, renewed_out, momentum_out,
    h_all, u_all, w, m1, m2, g, om,
    x_in, z_out, z_in, acc, spread, grad, p_own, p_out, p_in, y_out, y_in,
    val, mer, ren, mom,
    local_sem, store_sem, merged_sem,
    h_send, h_recv, u_send, u_recv, p_send, p_recv,
    x_send, x_recv, z_send, z_recv, gz_send, gz_recv, gx_send, gx_recv,
):
    tokens, width = hidden.shape[1:]
    block, columns = weights.shape[1:]
    rows = block // reps
    layers = reps // 2
    half = columns // HALVES
    factor = float(width) ** (-0.5)

    me_rep = lax.axis_index("rep")
    me_shard = lax.axis_index("fsdp")
    z, x = me_rep // 2, me_rep % 2
    y, core = me_shard // 2, me_shard % 2
    sibling = y * 2 + (1 - core)
    across = (1 - y) * 2 + core
    diagonal = (1 - y) * 2 + (1 - core)
    shards = (me_shard, sibling, across, diagonal)
    x_peer = z * 2 + (1 - x)

    def layer(d):
        return (z + d + layers) % layers

    def at_shard(p):
        return (me_rep, p)

    def at_rep(r):
        return (r, me_shard)

    def row_block(owner):
        return pl.ds(pl.multiple_of(owner * rows, STRIP), rows)

    def cols(h):
        return pl.ds(h * half, half)

    def toks(j):
        return pl.ds(j * tokens, tokens)

    def remote(src, dst, send, recv, device):
        return pltpu.make_async_remote_copy(
            src_ref=src, dst_ref=dst, send_sem=send, recv_sem=recv,
            device_id=device, device_id_type=MESH,
        )

    loads = [
        (hidden.at[0, :, pl.ds(pl.multiple_of(me_shard * block, 128), block)], h_all.at[toks(0)]),
        (weights.at[0], w),
        (upstream.at[0], u_all.at[toks(0)]),
        (global_params.at[0], g),
        (outer_momentum.at[0], om),
        (moment_one.at[0], m1),
        (moment_two.at[0], m2),
    ]
    loads = [pltpu.make_async_copy(a, b, local_sem.at[i]) for i, (a, b) in enumerate(loads)]
    for copy in loads:
        copy.start()

    barrier = pltpu.get_barrier_semaphore()
    greeted = [at_shard(p) for p in shards[1:]] + [at_rep(x_peer)]
    greeted += [at_rep(layer(d) * 2 + x) for d in range(1, layers)]
    for device in greeted:
        pl.semaphore_signal(barrier, inc=1, device_id=device, device_id_type=MESH)
    pl.semaphore_wait(barrier, len(greeted))

    sent = []

    def go(copy):
        copy.start()
        sent.append(copy)

    def send_hidden(j):
        part = hidden.at[0, :, pl.ds(pl.multiple_of(shards[j] * block, 128), block)]
        go(remote(part, h_all.at[toks(j)], h_send.at[j - 1], h_recv.at[j - 1], at_shard(shards[j])))

    def hidden_in(j):
        dst = h_all.at[toks(j)]
        remote(dst, dst, h_send.at[j - 1], h_recv.at[j - 1], at_shard(shards[j])).wait_recv()

    def send_upstream(j):
        go(remote(upstream.at[0], u_all.at[toks(j)], u_send.at[j - 1], u_recv.at[j - 1], at_shard(shards[j])))

    def upstream_in(j):
        dst = u_all.at[toks(j)]
        remote(dst, dst, u_send.at[j - 1], u_recv.at[j - 1], at_shard(shards[j])).wait_recv()

    order = tuple(range(1, layers)) + (0,)
    send_hidden(3)
    send_hidden(2)
    for h in range(HALVES):
        for d in order:
            part = weights.at[0, row_block(layer(d) * 2 + (1 - x)), cols(h)]
            go(remote(part, x_in.at[d, :, cols(h)], x_send.at[h, d], x_recv.at[h, d], at_rep(x_peer)))
    send_hidden(1)
    send_upstream(1)
    send_upstream(2)

    def project(j, dst):
        @pl.loop(0, columns // 256)
        def _(n):
            at = pl.ds(pl.multiple_of(n * 256, 256), 256)
            dst[:, at] = jnp.dot(h_all[toks(j), :], w[:, at], preferred_element_type=F32)

    loads[0].wait()
    loads[1].wait()
    project(0, p_own)
    hidden_in(1)
    project(1, p_out.at[0])
    go(remote(p_out.at[0], p_in.at[0], p_send.at[0], p_recv.at[0], at_shard(sibling)))

    for h in range(HALVES):
        for d in order:
            dst = x_in.at[d, :, cols(h)]
            remote(dst, dst, x_send.at[h, d], x_recv.at[h, d], at_rep(x_peer)).wait_recv()
            base = (layer(d) * 2 + x) * rows

            def pair(i, d=d, h=h, base=base):
                here = pl.ds(pl.multiple_of(base + i, STRIP), STRIP)
                total = w[here, cols(h)].astype(F32) + x_in[d, pl.ds(i, STRIP), cols(h)].astype(F32)
                if d == 0:
                    acc[pl.ds(i, STRIP), cols(h)] = total
                else:
                    z_out[d - 1, pl.ds(i, STRIP), cols(h)] = total.astype(BF16)

            strips(rows, pair)
            if d:
                go(remote(
                    z_out.at[d - 1, :, cols(h)], z_in.at[d - 1, :, cols(h)],
                    z_send.at[h, d - 1], z_recv.at[h, d - 1], at_rep(layer(d) * 2 + x),
                ))

    loads[3].wait()
    loads[4].wait()
    stores = []
    for h in range(HALVES):
        for d in range(1, layers):
            dst = z_in.at[d - 1, :, cols(h)]
            remote(dst, dst, z_send.at[h, d - 1], z_recv.at[h, d - 1], at_rep(me_rep)).wait_recv()

        def outer(i, h=h):
            here = pl.ds(i, STRIP)
            summed = acc[here, cols(h)]
            for d in range(1, layers):
                summed = summed + z_in[d - 1, here, cols(h)].astype(F32)
            now = g[here, cols(h)]
            pseudo = now - summed / reps
            momentum = outer_mu * om[here, cols(h)] + pseudo
            renewed = now - outer_rate * (pseudo + outer_mu * momentum)
            mom[here, cols(h)] = momentum
            ren[here, cols(h)] = renewed
            at = pl.ds(pl.multiple_of(me_rep * rows + i, STRIP), STRIP)
            spread[at, cols(h)] = renewed.astype(BF16)

        strips(rows, outer)
        own = spread.at[row_block(me_rep), cols(h)]
        go(remote(own, own, gx_send.at[h, 0], gx_recv.at[h, 0], at_rep(x_peer)))
        for d in order[:-1]:
            go(remote(own, own, gz_send.at[h, d - 1], gz_recv.at[h, d - 1], at_rep(layer(d) * 2 + x)))
    stores.append(pltpu.make_async_copy(ren, renewed_out.at[0], store_sem.at[0]))
    stores.append(pltpu.make_async_copy(mom, momentum_out.at[0], store_sem.at[1]))
    stores[0].start()
    stores[1].start()

    hidden_in(3)
    project(3, p_out.at[1])
    go(remote(p_out.at[1], p_in.at[1], p_send.at[1], p_recv.at[1], at_shard(sibling)))
    hidden_in(2)

    @pl.loop(0, columns // 256)
    def _(n):
        at = pl.ds(pl.multiple_of(n * 256, 256), 256)
        grad[pl.ds(0, tokens), at] = jnp.dot(h_all[toks(2), :], w[:, at], preferred_element_type=F32)

    remote(p_in.at[1], p_in.at[1], p_send.at[1], p_recv.at[1], at_shard(sibling)).wait_recv()

    def chip_sum(i):
        here = pl.ds(i, STRIP)
        y_out[here, :] = (grad[here, :] + p_in[1, here, :]).astype(BF16)

    strips(tokens, chip_sum)
    go(remote(y_out, y_in, p_send.at[2], p_recv.at[2], at_shard(across)))

    def forward(h, d):
        part = spread.at[row_block(layer(-d) * 2 + x), cols(h)]
        remote(part, part, gz_send.at[h, d - 1], gz_recv.at[h, d - 1], at_rep(me_rep)).wait_recv()
        go(remote(part, part, gx_send.at[h, d], gx_recv.at[h, d], at_rep(x_peer)))

    upstream_in(2)
    go(remote(u_all.at[toks(2)], u_all.at[toks(3)], u_send.at[2], u_recv.at[2], at_shard(sibling)))
    near_first = (1,) + tuple(range(layers - 1, 1, -1))
    for d in near_first:
        forward(0, d)
    loads[2].wait()
    loads[5].wait()
    loads[6].wait()
    upstream_in(1)
    upstream_in(3)

    part_rows = block // 3

    def inner(part):
        lhs = h_all[:, pl.ds(part * part_rows, part_rows)]
        base = part * part_rows

        @pl.loop(0, columns // 256)
        def _(n):
            at = pl.ds(pl.multiple_of(n * 256, 256), 256)
            grad[pl.ds(base, part_rows), at] = lax.dot_general(
                lhs, u_all[:, at], (((0,), (0,)), ((), ())), preferred_element_type=F32
            )

        def step(i):
            here = pl.ds(pl.multiple_of(base + i, STRIP), STRIP)
            updated = inner_step(
                grad[here, :] * factor, m1[here, :].astype(F32), m2[here, :].astype(F32), w[here, :].astype(F32)
            )
            grad[here, :] = mixing * updated

        strips(part_rows, step)

    inner(0)
    for d in near_first:
        forward(1, d)
    inner(1)
    inner(2)

    remote(p_in.at[0], p_in.at[0], p_send.at[0], p_recv.at[0], at_shard(sibling)).wait_recv()
    remote(y_in, y_in, p_send.at[2], p_recv.at[2], at_shard(across)).wait_recv()

    def finish(i):
        here = pl.ds(i, STRIP)
        total = p_own[here, :] + p_in[0, here, :] + y_in[here, :].astype(F32)
        val[here, :] = (total * factor).astype(BF16)

    strips(tokens, finish)
    stores.append(pltpu.make_async_copy(val, values_out.at[0], store_sem.at[2]))
    stores[2].start()

    def merge(owner, slot):
        base = owner * rows

        def body(i):
            here = pl.ds(pl.multiple_of(base + i, STRIP), STRIP)
            mer[here, :] = (grad[here, :] + (1.0 - mixing) * spread[here, :].astype(F32)).astype(BF16)

        strips(rows, body)
        copy = pltpu.make_async_copy(
            mer.at[row_block(owner)], merged_out.at[0, row_block(owner)], merged_sem.at[slot]
        )
        copy.start()
        stores.append(copy)

    merge(me_rep, 0)
    for i, d in enumerate(near_first):
        merge(layer(-d) * 2 + x, i + 1)
    for i, d in enumerate((0,) + near_first):
        owner = layer(-d) * 2 + (1 - x)
        for h in range(HALVES):
            part = spread.at[row_block(owner), cols(h)]
            remote(part, part, gx_send.at[h, d], gx_recv.at[h, d], at_rep(x_peer)).wait_recv()
        merge(owner, layers + i)

    for copy in sent:
        copy.wait_send()
    for copy in stores:
        copy.wait()


def fused_call(reps, hidden, upstream, weights, moment_one, moment_two, global_params, outer_momentum):
    tokens = hidden.shape[1]
    block, columns = weights.shape[1:]
    rows = block // reps
    layers = reps // 2
    dma = pltpu.SemaphoreType.DMA
    scratch = [
        pltpu.VMEM((4 * tokens, block), BF16),
        pltpu.VMEM((4 * tokens, columns), BF16),
        pltpu.VMEM((block, columns), BF16),
        pltpu.VMEM((block, columns), BF16),
        pltpu.VMEM((block, columns), BF16),
        pltpu.VMEM((rows, columns), F32),
        pltpu.VMEM((rows, columns), F32),
        pltpu.VMEM((layers, rows, columns), BF16),
        pltpu.VMEM((layers - 1, rows, columns), BF16),
        pltpu.VMEM((layers - 1, rows, columns), BF16),
        pltpu.VMEM((rows, columns), F32),
        pltpu.VMEM((block, columns), BF16),
        pltpu.VMEM((block, columns), F32),
        pltpu.VMEM((tokens, columns), F32),
        pltpu.VMEM((2, tokens, columns), F32),
        pltpu.VMEM((2, tokens, columns), F32),
        pltpu.VMEM((tokens, columns), BF16),
        pltpu.VMEM((tokens, columns), BF16),
        pltpu.VMEM((tokens, columns), BF16),
        pltpu.VMEM((block, columns), BF16),
        pltpu.VMEM((rows, columns), F32),
        pltpu.VMEM((rows, columns), F32),
        dma((7,)), dma((3,)), dma((reps,)),
        dma((3,)), dma((3,)), dma((3,)), dma((3,)), dma((3,)), dma((3,)),
        dma((HALVES, layers)), dma((HALVES, layers)),
        dma((HALVES, layers - 1)), dma((HALVES, layers - 1)),
        dma((HALVES, layers - 1)), dma((HALVES, layers - 1)),
        dma((HALVES, layers)), dma((HALVES, layers)),
    ]
    anywhere = pl.BlockSpec(memory_space=pl.ANY)
    return pl.pallas_call(
        functools.partial(fused, reps),
        out_shape=(
            jax.ShapeDtypeStruct((1, tokens, columns), BF16),
            jax.ShapeDtypeStruct(weights.shape, BF16),
            jax.ShapeDtypeStruct(global_params.shape, F32),
            jax.ShapeDtypeStruct(global_params.shape, F32),
        ),
        in_specs=[anywhere] * 7,
        out_specs=[anywhere] * 4,
        scratch_shapes=scratch,
        compiler_params=pltpu.CompilerParams(
            collective_id=0, has_side_effects=True, vmem_limit_bytes=56 * 1024 * 1024
        ),
        cost_estimate=pl.CostEstimate(
            flops=4 * tokens * hidden.shape[2] * columns, bytes_accessed=18 * 1024 * 1024, transcendentals=0
        ),
    )(hidden, upstream, weights, moment_one, moment_two, global_params, outer_momentum)


def collective_form(hidden, upstream, weights, moment_one, moment_two, global_params, outer_momentum):
    factor = float(hidden.shape[2]) ** (-0.5)
    tokens, grads_in = hidden[0], upstream[0]
    gathered = lax.all_gather(weights, "fsdp", axis=1, tiled=True)[0]
    values = (jnp.dot(tokens, gathered, preferred_element_type=F32) * factor).astype(BF16)
    partial = lax.dot_general(tokens, grads_in, (((0,), (0,)), ((), ())), preferred_element_type=F32)
    gradient = lax.psum_scatter(
        (partial * factor).astype(BF16), "fsdp", scatter_dimension=0, tiled=True
    ).astype(F32)
    updated = inner_step(
        gradient, moment_one[0].astype(F32), moment_two[0].astype(F32), weights[0].astype(F32)
    )
    owned = lax.psum_scatter(weights.astype(F32), "rep", scatter_dimension=1, tiled=True)
    pseudo = global_params - owned / lax.axis_size("rep")
    momentum = outer_mu * outer_momentum + pseudo
    renewed = global_params - outer_rate * (pseudo + outer_mu * momentum)
    spread = lax.all_gather(renewed.astype(BF16), "rep", axis=1, tiled=True).astype(F32)[0]
    merged = (mixing * updated + (1.0 - mixing) * spread).astype(BF16)
    return (values[None], merged[None], renewed, momentum)


def solution(mesh):
    reps, shards = mesh.shape["rep"], mesh.shape["fsdp"]

    def on_device(*arrays):
        rows = arrays[5].shape[1]
        if shards == 4 and reps % 2 == 0 and reps > 2 and rows % STRIP == 0:
            return fused_call(reps, *arrays)
        return collective_form(*arrays)

    return jax.shard_map(
        on_device,
        mesh=mesh,
        in_specs=(P("rep", "fsdp", None),) * 5 + (P("fsdp", "rep", None),) * 2,
        out_specs=(P("rep", "fsdp", None),) * 2 + (P("fsdp", "rep", None),) * 2,
        check_vma=False,
    )
```

```python
import functools

import jax
import jax.numpy as jnp
from jax import lax
from jax.experimental import pallas as pl
from jax.experimental.pallas import tpu as pltpu
from jax.sharding import PartitionSpec as P

beta_one = 0.9
beta_two = 0.95
bias_one = 1.0 - 0.9**8
bias_two = 1.0 - 0.95**8
inner_rate = 0.25
decay_rate = 0.1
epsilon = 1e-08
outer_rate = 0.7
outer_mu = 0.9
mixing = 0.5

MESH = pl.DeviceIdType.MESH
BF16 = jnp.bfloat16
F32 = jnp.float32
CHUNKS = 4
AHEAD = 4
STRIP = 16


def inner_step(gradient, first, second, current):
    moment_new = beta_one * first + (1.0 - beta_one) * gradient
    second_new = beta_two * second + (1.0 - beta_two) * gradient * gradient
    stepped = moment_new / bias_one / (jnp.sqrt(second_new / bias_two) + epsilon)
    return current - inner_rate * (stepped + decay_rate * current)


def strips(rows, body, tall=STRIP):
    @pl.loop(0, rows // tall)
    def _(i):
        body(pl.multiple_of(i * tall, STRIP))


def fused(
    reps,
    hidden, upstream, weights, moment_one, moment_two, global_params, outer_momentum,
    values_out, merged_out, renewed_out, momentum_out,
    h_all, u_all, w, m1, m2, g, om,
    x_in, z_out, z_in, acc, spread, grad, p_own, p_out, p_in, y_out, y_in,
    val, mer, ren, mom,
    local_sem, store_sem, merged_sem,
    h_send, h_recv, u_send, u_recv, p_send, p_recv,
    x_send, x_recv, z_send, z_recv, gz_send, gz_recv, gx_send, gx_recv,
):
    tokens, width = hidden.shape[1:]
    block, columns = weights.shape[1:]
    rows = block // reps
    layers = reps // 2
    wide = columns // CHUNKS
    factor = float(width) ** (-0.5)

    me_rep = lax.axis_index("rep")
    me_shard = lax.axis_index("fsdp")
    z, x = me_rep // 2, me_rep % 2
    y, core = me_shard // 2, me_shard % 2
    sibling = y * 2 + (1 - core)
    across = (1 - y) * 2 + core
    diagonal = (1 - y) * 2 + (1 - core)
    shards = (me_shard, sibling, across, diagonal)
    x_peer = z * 2 + (1 - x)

    def layer(d):
        return (z + d + layers) % layers

    def at_shard(p):
        return (me_rep, p)

    def at_rep(r):
        return (r, me_shard)

    def row_block(owner):
        return pl.ds(pl.multiple_of(owner * rows, STRIP), rows)

    def cols(h):
        return pl.ds(h * wide, wide)

    def toks(j):
        return pl.ds(j * tokens, tokens)

    def remote(src, dst, send, recv, device):
        return pltpu.make_async_remote_copy(
            src_ref=src, dst_ref=dst, send_sem=send, recv_sem=recv,
            device_id=device, device_id_type=MESH,
        )

    loads = [
        (hidden.at[0, :, pl.ds(pl.multiple_of(me_shard * block, 128), block)], h_all.at[toks(0)]),
        (weights.at[0], w),
        (upstream.at[0], u_all.at[toks(0)]),
        (global_params.at[0], g),
        (outer_momentum.at[0], om),
        (moment_one.at[0], m1),
        (moment_two.at[0], m2),
    ]
    loads = [pltpu.make_async_copy(a, b, local_sem.at[i]) for i, (a, b) in enumerate(loads)]
    for copy in loads:
        copy.start()

    barrier = pltpu.get_barrier_semaphore()
    greeted = [at_shard(p) for p in shards[1:]] + [at_rep(x_peer)]
    greeted += [at_rep(layer(d) * 2 + x) for d in range(1, layers)]
    for device in greeted:
        pl.semaphore_signal(barrier, inc=1, device_id=device, device_id_type=MESH)
    pl.semaphore_wait(barrier, len(greeted))

    sent = []

    def go(copy):
        copy.start()
        sent.append(copy)

    def send_hidden(j):
        part = hidden.at[0, :, pl.ds(pl.multiple_of(shards[j] * block, 128), block)]
        go(remote(part, h_all.at[toks(j)], h_send.at[j - 1], h_recv.at[j - 1], at_shard(shards[j])))

    def hidden_in(j):
        dst = h_all.at[toks(j)]
        remote(dst, dst, h_send.at[j - 1], h_recv.at[j - 1], at_shard(shards[j])).wait_recv()

    def send_upstream(j):
        go(remote(upstream.at[0], u_all.at[toks(j)], u_send.at[j - 1], u_recv.at[j - 1], at_shard(shards[j])))

    def upstream_in(j):
        dst = u_all.at[toks(j)]
        remote(dst, dst, u_send.at[j - 1], u_recv.at[j - 1], at_shard(shards[j])).wait_recv()

    order = tuple(range(1, layers)) + (0,)
    pieces = [(h, d) for h in range(CHUNKS) for d in order]

    def send_piece(h, d):
        part = weights.at[0, row_block(layer(d) * 2 + (1 - x)), cols(h)]
        go(remote(part, x_in.at[d, :, cols(h)], x_send.at[h, d], x_recv.at[h, d], at_rep(x_peer)))

    for piece in pieces[:AHEAD]:
        send_piece(*piece)
    send_hidden(3)
    send_hidden(2)
    send_hidden(1)
    send_upstream(1)
    send_upstream(2)

    def project(j, dst):
        @pl.loop(0, columns // 256)
        def _(n):
            at = pl.ds(pl.multiple_of(n * 256, 256), 256)
            dst[:, at] = jnp.dot(h_all[toks(j), :], w[:, at], preferred_element_type=F32)

    loads[0].wait()
    loads[1].wait()
    project(0, p_own)
    hidden_in(1)
    project(1, p_out.at[0])
    go(remote(p_out.at[0], p_in.at[0], p_send.at[0], p_recv.at[0], at_shard(sibling)))

    tall = rows // 3 if rows % 48 == 0 else STRIP

    def pairs(h):
        for d in order:
            dst = x_in.at[d, :, cols(h)]
            remote(dst, dst, x_send.at[h, d], x_recv.at[h, d], at_rep(x_peer)).wait_recv()
            later = h * layers + order.index(d) + AHEAD
            if later < len(pieces):
                send_piece(*pieces[later])
            base = (layer(d) * 2 + x) * rows

            def pair(i, d=d, base=base):
                here = pl.ds(pl.multiple_of(base + i, STRIP), tall)
                total = w[here, cols(h)].astype(F32) + x_in[d, pl.ds(i, tall), cols(h)].astype(F32)
                if d == 0:
                    acc[pl.ds(i, tall), cols(h)] = total
                else:
                    z_out[d - 1, pl.ds(i, tall), cols(h)] = total.astype(BF16)

            strips(rows, pair, tall)
            if d:
                go(remote(
                    z_out.at[d - 1, :, cols(h)], z_in.at[d - 1, :, cols(h)],
                    z_send.at[h, d - 1], z_recv.at[h, d - 1], at_rep(layer(d) * 2 + x),
                ))

    def renew(h):
        for d in range(1, layers):
            dst = z_in.at[d - 1, :, cols(h)]
            remote(dst, dst, z_send.at[h, d - 1], z_recv.at[h, d - 1], at_rep(me_rep)).wait_recv()

        def outer(i):
            here = pl.ds(i, tall)
            summed = acc[here, cols(h)]
            for d in range(1, layers):
                summed = summed + z_in[d - 1, here, cols(h)].astype(F32)
            now = g[here, cols(h)]
            pseudo = now - summed / reps
            momentum = outer_mu * om[here, cols(h)] + pseudo
            renewed = now - outer_rate * (pseudo + outer_mu * momentum)
            mom[here, cols(h)] = momentum
            ren[here, cols(h)] = renewed
            at = pl.ds(pl.multiple_of(me_rep * rows + i, STRIP), tall)
            spread[at, cols(h)] = renewed.astype(BF16)

        strips(rows, outer, tall)
        own = spread.at[row_block(me_rep), cols(h)]
        for d in order[:-1]:
            go(remote(own, own, gz_send.at[h, d - 1], gz_recv.at[h, d - 1], at_rep(layer(d) * 2 + x)))
        go(remote(own, own, gx_send.at[h, 0], gx_recv.at[h, 0], at_rep(x_peer)))

    near_first = (1,) + tuple(range(layers - 1, 1, -1))

    def forward(h):
        for d in near_first:
            part = spread.at[row_block(layer(-d) * 2 + x), cols(h)]
            remote(part, part, gz_send.at[h, d - 1], gz_recv.at[h, d - 1], at_rep(me_rep)).wait_recv()
            go(remote(part, part, gx_send.at[h, d], gx_recv.at[h, d], at_rep(x_peer)))

    loads[3].wait()
    loads[4].wait()
    pairs(0)
    pairs(1)
    renew(0)
    pairs(2)
    renew(1)
    forward(0)
    pairs(3)
    renew(2)
    forward(1)
    renew(3)
    stores = [
        pltpu.make_async_copy(ren, renewed_out.at[0], store_sem.at[0]),
        pltpu.make_async_copy(mom, momentum_out.at[0], store_sem.at[1]),
    ]
    stores[0].start()
    stores[1].start()

    hidden_in(3)
    project(3, p_out.at[1])
    go(remote(p_out.at[1], p_in.at[1], p_send.at[1], p_recv.at[1], at_shard(sibling)))
    hidden_in(2)

    @pl.loop(0, columns // 256)
    def _(n):
        at = pl.ds(pl.multiple_of(n * 256, 256), 256)
        grad[pl.ds(0, tokens), at] = jnp.dot(h_all[toks(2), :], w[:, at], preferred_element_type=F32)

    remote(p_in.at[1], p_in.at[1], p_send.at[1], p_recv.at[1], at_shard(sibling)).wait_recv()

    def chip_sum(i):
        here = pl.ds(i, STRIP)
        y_out[here, :] = (grad[here, :] + p_in[1, here, :]).astype(BF16)

    strips(tokens, chip_sum)
    go(remote(y_out, y_in, p_send.at[2], p_recv.at[2], at_shard(across)))

    upstream_in(2)
    go(remote(u_all.at[toks(2)], u_all.at[toks(3)], u_send.at[2], u_recv.at[2], at_shard(sibling)))
    forward(2)
    loads[2].wait()
    loads[5].wait()
    loads[6].wait()
    upstream_in(1)
    upstream_in(3)

    part_rows = block // 3

    def inner(part):
        lhs = h_all[:, pl.ds(part * part_rows, part_rows)]
        base = part * part_rows

        @pl.loop(0, columns // 256)
        def _(n):
            at = pl.ds(pl.multiple_of(n * 256, 256), 256)
            grad[pl.ds(base, part_rows), at] = lax.dot_general(
                lhs, u_all[:, at], (((0,), (0,)), ((), ())), preferred_element_type=F32
            )

        def step(i):
            here = pl.ds(pl.multiple_of(base + i, STRIP), STRIP)
            updated = inner_step(
                grad[here, :] * factor, m1[here, :].astype(F32), m2[here, :].astype(F32), w[here, :].astype(F32)
            )
            grad[here, :] = mixing * updated

        strips(part_rows, step)

    inner(0)
    forward(3)
    inner(1)
    inner(2)

    remote(p_in.at[0], p_in.at[0], p_send.at[0], p_recv.at[0], at_shard(sibling)).wait_recv()
    remote(y_in, y_in, p_send.at[2], p_recv.at[2], at_shard(across)).wait_recv()

    def finish(i):
        here = pl.ds(i, STRIP)
        total = p_own[here, :] + p_in[0, here, :] + y_in[here, :].astype(F32)
        val[here, :] = (total * factor).astype(BF16)

    strips(tokens, finish)
    stores.append(pltpu.make_async_copy(val, values_out.at[0], store_sem.at[2]))
    stores[2].start()

    def merge(owner, slot):
        base = owner * rows

        def body(i):
            here = pl.ds(pl.multiple_of(base + i, STRIP), STRIP)
            mer[here, :] = (grad[here, :] + (1.0 - mixing) * spread[here, :].astype(F32)).astype(BF16)

        strips(rows, body)
        copy = pltpu.make_async_copy(
            mer.at[row_block(owner)], merged_out.at[0, row_block(owner)], merged_sem.at[slot]
        )
        copy.start()
        stores.append(copy)

    merge(me_rep, 0)
    for i, d in enumerate(near_first):
        merge(layer(-d) * 2 + x, i + 1)
    for i, d in enumerate((0,) + near_first):
        owner = layer(-d) * 2 + (1 - x)
        for h in range(CHUNKS):
            part = spread.at[row_block(owner), cols(h)]
            remote(part, part, gx_send.at[h, d], gx_recv.at[h, d], at_rep(x_peer)).wait_recv()
        merge(owner, layers + i)

    for copy in sent:
        copy.wait_send()
    for copy in stores:
        copy.wait()


def fused_call(reps, hidden, upstream, weights, moment_one, moment_two, global_params, outer_momentum):
    tokens = hidden.shape[1]
    block, columns = weights.shape[1:]
    rows = block // reps
    layers = reps // 2
    dma = pltpu.SemaphoreType.DMA
    scratch = [
        pltpu.VMEM((4 * tokens, block), BF16),
        pltpu.VMEM((4 * tokens, columns), BF16),
        pltpu.VMEM((block, columns), BF16),
        pltpu.VMEM((block, columns), BF16),
        pltpu.VMEM((block, columns), BF16),
        pltpu.VMEM((rows, columns), F32),
        pltpu.VMEM((rows, columns), F32),
        pltpu.VMEM((layers, rows, columns), BF16),
        pltpu.VMEM((layers - 1, rows, columns), BF16),
        pltpu.VMEM((layers - 1, rows, columns), BF16),
        pltpu.VMEM((rows, columns), F32),
        pltpu.VMEM((block, columns), BF16),
        pltpu.VMEM((block, columns), F32),
        pltpu.VMEM((tokens, columns), F32),
        pltpu.VMEM((2, tokens, columns), F32),
        pltpu.VMEM((2, tokens, columns), F32),
        pltpu.VMEM((tokens, columns), BF16),
        pltpu.VMEM((tokens, columns), BF16),
        pltpu.VMEM((tokens, columns), BF16),
        pltpu.VMEM((block, columns), BF16),
        pltpu.VMEM((rows, columns), F32),
        pltpu.VMEM((rows, columns), F32),
        dma((7,)), dma((3,)), dma((reps,)),
        dma((3,)), dma((3,)), dma((3,)), dma((3,)), dma((3,)), dma((3,)),
        dma((CHUNKS, layers)), dma((CHUNKS, layers)),
        dma((CHUNKS, layers - 1)), dma((CHUNKS, layers - 1)),
        dma((CHUNKS, layers - 1)), dma((CHUNKS, layers - 1)),
        dma((CHUNKS, layers)), dma((CHUNKS, layers)),
    ]
    anywhere = pl.BlockSpec(memory_space=pl.ANY)
    return pl.pallas_call(
        functools.partial(fused, reps),
        out_shape=(
            jax.ShapeDtypeStruct((1, tokens, columns), BF16),
            jax.ShapeDtypeStruct(weights.shape, BF16),
            jax.ShapeDtypeStruct(global_params.shape, F32),
            jax.ShapeDtypeStruct(global_params.shape, F32),
        ),
        in_specs=[anywhere] * 7,
        out_specs=[anywhere] * 4,
        scratch_shapes=scratch,
        compiler_params=pltpu.CompilerParams(
            collective_id=0, has_side_effects=True, vmem_limit_bytes=56 * 1024 * 1024
        ),
        cost_estimate=pl.CostEstimate(
            flops=4 * tokens * hidden.shape[2] * columns, bytes_accessed=18 * 1024 * 1024, transcendentals=0
        ),
    )(hidden, upstream, weights, moment_one, moment_two, global_params, outer_momentum)


def collective_form(hidden, upstream, weights, moment_one, moment_two, global_params, outer_momentum):
    factor = float(hidden.shape[2]) ** (-0.5)
    tokens, grads_in = hidden[0], upstream[0]
    gathered = lax.all_gather(weights, "fsdp", axis=1, tiled=True)[0]
    values = (jnp.dot(tokens, gathered, preferred_element_type=F32) * factor).astype(BF16)
    partial = lax.dot_general(tokens, grads_in, (((0,), (0,)), ((), ())), preferred_element_type=F32)
    gradient = lax.psum_scatter(
        (partial * factor).astype(BF16), "fsdp", scatter_dimension=0, tiled=True
    ).astype(F32)
    updated = inner_step(
        gradient, moment_one[0].astype(F32), moment_two[0].astype(F32), weights[0].astype(F32)
    )
    owned = lax.psum_scatter(weights.astype(F32), "rep", scatter_dimension=1, tiled=True)
    pseudo = global_params - owned / lax.axis_size("rep")
    momentum = outer_mu * outer_momentum + pseudo
    renewed = global_params - outer_rate * (pseudo + outer_mu * momentum)
    spread = lax.all_gather(renewed.astype(BF16), "rep", axis=1, tiled=True).astype(F32)[0]
    merged = (mixing * updated + (1.0 - mixing) * spread).astype(BF16)
    return (values[None], merged[None], renewed, momentum)


def solution(mesh):
    reps, shards = mesh.shape["rep"], mesh.shape["fsdp"]

    def on_device(*arrays):
        rows = arrays[5].shape[1]
        if shards == 4 and reps % 2 == 0 and reps > 2 and rows % STRIP == 0:
            return fused_call(reps, *arrays)
        return collective_form(*arrays)

    return jax.shard_map(
        on_device,
        mesh=mesh,
        in_specs=(P("rep", "fsdp", None),) * 5 + (P("fsdp", "rep", None),) * 2,
        out_specs=(P("rep", "fsdp", None),) * 2 + (P("fsdp", "rep", None),) * 2,
        check_vma=False,
    )
```

```python
import functools

import jax
import jax.numpy as jnp
from jax import lax
from jax.experimental import pallas as pl
from jax.experimental.pallas import tpu as pltpu
from jax.sharding import PartitionSpec as P

beta_one = 0.9
beta_two = 0.95
bias_one = 1.0 - 0.9**8
bias_two = 1.0 - 0.95**8
inner_rate = 0.25
decay_rate = 0.1
epsilon = 1e-08
outer_rate = 0.7
outer_mu = 0.9
mixing = 0.5

MESH = pl.DeviceIdType.MESH
BF16 = jnp.bfloat16
F32 = jnp.float32
CHUNKS = 4
AHEAD = 4
STRIP = 16


def inner_step(gradient, first, second, current):
    moment_new = beta_one * first + (1.0 - beta_one) * gradient
    second_new = beta_two * second + (1.0 - beta_two) * gradient * gradient
    stepped = moment_new / bias_one / (jnp.sqrt(second_new / bias_two) + epsilon)
    return current - inner_rate * (stepped + decay_rate * current)


def half_inner(raw, first, second, current, factor):
    scale = mixing * inner_rate / bias_one
    moment = (scale * beta_one) * first + (scale * (1.0 - beta_one) * factor) * raw
    second_new = (beta_two / bias_two) * second + ((1.0 - beta_two) * factor * factor / bias_two) * (raw * raw)
    return (mixing * (1.0 - inner_rate * decay_rate)) * current - moment / (jnp.sqrt(second_new) + epsilon)


def strips(rows, body, tall=STRIP):
    @pl.loop(0, rows // tall)
    def _(i):
        body(pl.multiple_of(i * tall, STRIP))


def fused(
    reps,
    hidden, upstream, weights, moment_one, moment_two, global_params, outer_momentum,
    values_out, merged_out, renewed_out, momentum_out,
    h_all, h_t, u_all, w, m1, m2, g, om,
    x_in, z_out, z_in, acc, spread, grad, p_own, p_far, p_out, p_in, y_out, y_in,
    val, mer, ren, mom,
    local_sem, store_sem, merged_sem,
    h_send, h_recv, u_send, u_recv, p_send, p_recv,
    x_send, x_recv, z_send, z_recv, gz_send, gz_recv, gx_send, gx_recv,
):
    tokens, width = hidden.shape[1:]
    block, columns = weights.shape[1:]
    rows = block // reps
    layers = reps // 2
    wide = columns // CHUNKS
    factor = float(width) ** (-0.5)

    me_rep = lax.axis_index("rep")
    me_shard = lax.axis_index("fsdp")
    z, x = me_rep // 2, me_rep % 2
    y, core = me_shard // 2, me_shard % 2
    sibling = y * 2 + (1 - core)
    across = (1 - y) * 2 + core
    diagonal = (1 - y) * 2 + (1 - core)
    shards = (me_shard, sibling, across, diagonal)
    x_peer = z * 2 + (1 - x)

    def layer(d):
        return (z + d + layers) % layers

    def at_shard(p):
        return (me_rep, p)

    def at_rep(r):
        return (r, me_shard)

    def row_block(owner):
        return pl.ds(pl.multiple_of(owner * rows, STRIP), rows)

    def cols(h):
        return pl.ds(h * wide, wide)

    def toks(j):
        return pl.ds(j * tokens, tokens)

    def remote(src, dst, send, recv, device):
        return pltpu.make_async_remote_copy(
            src_ref=src, dst_ref=dst, send_sem=send, recv_sem=recv,
            device_id=device, device_id_type=MESH,
        )

    loads = [
        (hidden.at[0, :, pl.ds(pl.multiple_of(me_shard * block, 128), block)], h_all.at[toks(0)]),
        (weights.at[0], w),
        (upstream.at[0], u_all.at[toks(0)]),
        (global_params.at[0], g),
        (outer_momentum.at[0], om),
        (moment_one.at[0], m1),
        (moment_two.at[0], m2),
    ]
    loads = [pltpu.make_async_copy(a, b, local_sem.at[i]) for i, (a, b) in enumerate(loads)]
    for copy in loads:
        copy.start()

    barrier = pltpu.get_barrier_semaphore()
    greeted = [at_shard(p) for p in shards[1:]] + [at_rep(x_peer)]
    greeted += [at_rep(layer(d) * 2 + x) for d in range(1, layers)]
    for device in greeted:
        pl.semaphore_signal(barrier, inc=1, device_id=device, device_id_type=MESH)
    pl.semaphore_wait(barrier, len(greeted))

    sent = []

    def go(copy):
        copy.start()
        sent.append(copy)

    def send_hidden(j):
        part = hidden.at[0, :, pl.ds(pl.multiple_of(shards[j] * block, 128), block)]
        go(remote(part, h_all.at[toks(j)], h_send.at[j - 1], h_recv.at[j - 1], at_shard(shards[j])))

    def hidden_in(j):
        dst = h_all.at[toks(j)]
        remote(dst, dst, h_send.at[j - 1], h_recv.at[j - 1], at_shard(shards[j])).wait_recv()

    def send_upstream(j, h):
        go(remote(
            upstream.at[0, :, cols(h)], u_all.at[toks(j), cols(h)],
            u_send.at[j - 1, h], u_recv.at[j - 1, h], at_shard(shards[j]),
        ))

    def upstream_in(j, h):
        dst = u_all.at[toks(j), cols(h)]
        remote(dst, dst, u_send.at[j - 1, h], u_recv.at[j - 1, h], at_shard(shards[j])).wait_recv()

    def pass_upstream(h):
        upstream_in(2, h)
        go(remote(
            u_all.at[toks(2), cols(h)], u_all.at[toks(3), cols(h)],
            u_send.at[2, h], u_recv.at[2, h], at_shard(sibling),
        ))

    order = tuple(range(1, layers)) + (0,)
    pieces = [(h, d) for h in range(CHUNKS) for d in order]

    def send_piece(h, d):
        part = weights.at[0, row_block(layer(d) * 2 + (1 - x)), cols(h)]
        go(remote(part, x_in.at[d, :, cols(h)], x_send.at[h, d], x_recv.at[h, d], at_rep(x_peer)))

    for piece in pieces[:AHEAD]:
        send_piece(*piece)
    send_hidden(3)
    send_hidden(2)
    send_hidden(1)
    for h in range(CHUNKS):
        send_upstream(1, h)

    def project(j, dst):
        @pl.loop(0, columns // 256)
        def _(n):
            at = pl.ds(pl.multiple_of(n * 256, 256), 256)
            dst[:, at] = jnp.dot(h_all[toks(j), :], w[:, at], preferred_element_type=F32)

    def turn(j):
        @pl.loop(0, block // 128)
        def _(i):
            at = pl.ds(pl.multiple_of(i * 128, 128), 128)
            h_t[at, toks(j)] = h_all[toks(j), at].T

    loads[0].wait()
    loads[1].wait()
    project(0, p_own)
    turn(0)
    hidden_in(1)
    project(1, p_out.at[0])
    go(remote(p_out.at[0], p_in.at[0], p_send.at[0], p_recv.at[0], at_shard(sibling)))
    turn(1)

    tall = rows // 3 if rows % 48 == 0 else STRIP

    def pairs(h):
        for d in order:
            dst = x_in.at[d, :, cols(h)]
            remote(dst, dst, x_send.at[h, d], x_recv.at[h, d], at_rep(x_peer)).wait_recv()
            later = h * layers + order.index(d) + AHEAD
            if later < len(pieces):
                send_piece(*pieces[later])
            base = (layer(d) * 2 + x) * rows

            def pair(i, d=d, base=base):
                here = pl.ds(pl.multiple_of(base + i, STRIP), tall)
                total = w[here, cols(h)].astype(F32) + x_in[d, pl.ds(i, tall), cols(h)].astype(F32)
                if d == 0:
                    acc[pl.ds(i, tall), cols(h)] = total
                else:
                    z_out[d - 1, pl.ds(i, tall), cols(h)] = total.astype(BF16)

            strips(rows, pair, tall)
            if d:
                go(remote(
                    z_out.at[d - 1, :, cols(h)], z_in.at[d - 1, :, cols(h)],
                    z_send.at[h, d - 1], z_recv.at[h, d - 1], at_rep(layer(d) * 2 + x),
                ))

    def renew(h):
        for d in range(1, layers):
            dst = z_in.at[d - 1, :, cols(h)]
            remote(dst, dst, z_send.at[h, d - 1], z_recv.at[h, d - 1], at_rep(me_rep)).wait_recv()

        def outer(i):
            here = pl.ds(i, tall)
            summed = acc[here, cols(h)]
            for d in range(1, layers):
                summed = summed + z_in[d - 1, here, cols(h)].astype(F32)
            now = g[here, cols(h)]
            pseudo = now - summed / reps
            momentum = outer_mu * om[here, cols(h)] + pseudo
            renewed = now - outer_rate * (pseudo + outer_mu * momentum)
            mom[here, cols(h)] = momentum
            ren[here, cols(h)] = renewed
            at = pl.ds(pl.multiple_of(me_rep * rows + i, STRIP), tall)
            spread[at, cols(h)] = renewed.astype(BF16)

        strips(rows, outer, tall)
        own = spread.at[row_block(me_rep), cols(h)]
        for d in order[:-1]:
            go(remote(own, own, gz_send.at[h, d - 1], gz_recv.at[h, d - 1], at_rep(layer(d) * 2 + x)))
        go(remote(own, own, gx_send.at[h, 0], gx_recv.at[h, 0], at_rep(x_peer)))

    near_first = (1,) + tuple(range(layers - 1, 1, -1))

    def forward(h):
        for d in near_first:
            part = spread.at[row_block(layer(-d) * 2 + x), cols(h)]
            remote(part, part, gz_send.at[h, d - 1], gz_recv.at[h, d - 1], at_rep(me_rep)).wait_recv()
            go(remote(part, part, gx_send.at[h, d], gx_recv.at[h, d], at_rep(x_peer)))

    part_rows = block // 3
    high = 48 if block % 48 == 0 else STRIP

    def inner(h):
        upstream_in(1, h)
        upstream_in(3, h)

        @pl.loop(0, 3)
        def _(part):
            at = pl.ds(pl.multiple_of(part * part_rows, STRIP), part_rows)
            grad[at, cols(h)] = jnp.dot(h_t[at, :], u_all[:, cols(h)], preferred_element_type=F32)

        def step(i):
            here = (pl.ds(i, high), cols(h))
            grad[here] = half_inner(
                grad[here], m1[here].astype(F32), m2[here].astype(F32), w[here].astype(F32), factor
            )

        strips(block, step, high)

    loads[3].wait()
    loads[4].wait()
    pairs(0)
    pairs(1)
    renew(0)
    send_upstream(2, 0)
    pairs(2)
    renew(1)
    send_upstream(2, 1)
    forward(0)
    pairs(3)

    hidden_in(3)
    send_upstream(2, 2)
    send_upstream(2, 3)
    project(3, p_out.at[1])
    go(remote(p_out.at[1], p_in.at[1], p_send.at[1], p_recv.at[1], at_shard(sibling)))
    renew(2)
    hidden_in(2)
    project(2, p_far)
    remote(p_in.at[1], p_in.at[1], p_send.at[1], p_recv.at[1], at_shard(sibling)).wait_recv()

    def chip_sum(i):
        here = pl.ds(i, STRIP)
        y_out[here, :] = (p_far[here, :] + p_in[1, here, :]).astype(BF16)

    strips(tokens, chip_sum)
    go(remote(y_out, y_in, p_send.at[2], p_recv.at[2], at_shard(across)))
    forward(1)
    renew(3)
    stores = [
        pltpu.make_async_copy(ren, renewed_out.at[0], store_sem.at[0]),
        pltpu.make_async_copy(mom, momentum_out.at[0], store_sem.at[1]),
    ]
    stores[0].start()
    stores[1].start()
    turn(3)
    turn(2)
    loads[2].wait()
    loads[5].wait()
    loads[6].wait()
    pass_upstream(0)
    pass_upstream(1)
    inner(0)
    forward(2)
    pass_upstream(2)
    inner(1)
    pass_upstream(3)
    forward(3)
    inner(2)
    inner(3)

    remote(p_in.at[0], p_in.at[0], p_send.at[0], p_recv.at[0], at_shard(sibling)).wait_recv()
    remote(y_in, y_in, p_send.at[2], p_recv.at[2], at_shard(across)).wait_recv()

    def finish(i):
        here = pl.ds(i, STRIP)
        total = p_own[here, :] + p_in[0, here, :] + y_in[here, :].astype(F32)
        val[here, :] = (total * factor).astype(BF16)

    strips(tokens, finish)
    stores.append(pltpu.make_async_copy(val, values_out.at[0], store_sem.at[2]))
    stores[2].start()

    def merge(owner, slot):
        base = owner * rows

        def body(i):
            here = pl.ds(pl.multiple_of(base + i, STRIP), STRIP)
            mer[here, :] = (grad[here, :] + (1.0 - mixing) * spread[here, :].astype(F32)).astype(BF16)

        strips(rows, body)
        copy = pltpu.make_async_copy(
            mer.at[row_block(owner)], merged_out.at[0, row_block(owner)], merged_sem.at[slot]
        )
        copy.start()
        stores.append(copy)

    merge(me_rep, 0)
    for i, d in enumerate(near_first):
        merge(layer(-d) * 2 + x, i + 1)
    for i, d in enumerate((0,) + near_first):
        owner = layer(-d) * 2 + (1 - x)
        for h in range(CHUNKS):
            part = spread.at[row_block(owner), cols(h)]
            remote(part, part, gx_send.at[h, d], gx_recv.at[h, d], at_rep(x_peer)).wait_recv()
        merge(owner, layers + i)

    for copy in sent:
        copy.wait_send()
    for copy in stores:
        copy.wait()


def fused_call(reps, hidden, upstream, weights, moment_one, moment_two, global_params, outer_momentum):
    tokens = hidden.shape[1]
    block, columns = weights.shape[1:]
    rows = block // reps
    layers = reps // 2
    dma = pltpu.SemaphoreType.DMA
    scratch = [
        pltpu.VMEM((4 * tokens, block), BF16),
        pltpu.VMEM((block, 4 * tokens), BF16),
        pltpu.VMEM((4 * tokens, columns), BF16),
        pltpu.VMEM((block, columns), BF16),
        pltpu.VMEM((block, columns), BF16),
        pltpu.VMEM((block, columns), BF16),
        pltpu.VMEM((rows, columns), F32),
        pltpu.VMEM((rows, columns), F32),
        pltpu.VMEM((layers, rows, columns), BF16),
        pltpu.VMEM((layers - 1, rows, columns), BF16),
        pltpu.VMEM((layers - 1, rows, columns), BF16),
        pltpu.VMEM((rows, columns), F32),
        pltpu.VMEM((block, columns), BF16),
        pltpu.VMEM((block, columns), F32),
        pltpu.VMEM((tokens, columns), F32),
        pltpu.VMEM((tokens, columns), F32),
        pltpu.VMEM((2, tokens, columns), F32),
        pltpu.VMEM((2, tokens, columns), F32),
        pltpu.VMEM((tokens, columns), BF16),
        pltpu.VMEM((tokens, columns), BF16),
        pltpu.VMEM((tokens, columns), BF16),
        pltpu.VMEM((block, columns), BF16),
        pltpu.VMEM((rows, columns), F32),
        pltpu.VMEM((rows, columns), F32),
        dma((7,)), dma((3,)), dma((reps,)),
        dma((3,)), dma((3,)), dma((3, CHUNKS)), dma((3, CHUNKS)), dma((3,)), dma((3,)),
        dma((CHUNKS, layers)), dma((CHUNKS, layers)),
        dma((CHUNKS, layers - 1)), dma((CHUNKS, layers - 1)),
        dma((CHUNKS, layers - 1)), dma((CHUNKS, layers - 1)),
        dma((CHUNKS, layers)), dma((CHUNKS, layers)),
    ]
    anywhere = pl.BlockSpec(memory_space=pl.ANY)
    return pl.pallas_call(
        functools.partial(fused, reps),
        out_shape=(
            jax.ShapeDtypeStruct((1, tokens, columns), BF16),
            jax.ShapeDtypeStruct(weights.shape, BF16),
            jax.ShapeDtypeStruct(global_params.shape, F32),
            jax.ShapeDtypeStruct(global_params.shape, F32),
        ),
        in_specs=[anywhere] * 7,
        out_specs=[anywhere] * 4,
        scratch_shapes=scratch,
        compiler_params=pltpu.CompilerParams(
            collective_id=0, has_side_effects=True, vmem_limit_bytes=56 * 1024 * 1024
        ),
        cost_estimate=pl.CostEstimate(
            flops=4 * tokens * hidden.shape[2] * columns, bytes_accessed=18 * 1024 * 1024, transcendentals=0
        ),
    )(hidden, upstream, weights, moment_one, moment_two, global_params, outer_momentum)


def collective_form(hidden, upstream, weights, moment_one, moment_two, global_params, outer_momentum):
    factor = float(hidden.shape[2]) ** (-0.5)
    tokens, grads_in = hidden[0], upstream[0]
    gathered = lax.all_gather(weights, "fsdp", axis=1, tiled=True)[0]
    values = (jnp.dot(tokens, gathered, preferred_element_type=F32) * factor).astype(BF16)
    partial = lax.dot_general(tokens, grads_in, (((0,), (0,)), ((), ())), preferred_element_type=F32)
    gradient = lax.psum_scatter(
        (partial * factor).astype(BF16), "fsdp", scatter_dimension=0, tiled=True
    ).astype(F32)
    updated = inner_step(
        gradient, moment_one[0].astype(F32), moment_two[0].astype(F32), weights[0].astype(F32)
    )
    owned = lax.psum_scatter(weights.astype(F32), "rep", scatter_dimension=1, tiled=True)
    pseudo = global_params - owned / lax.axis_size("rep")
    momentum = outer_mu * outer_momentum + pseudo
    renewed = global_params - outer_rate * (pseudo + outer_mu * momentum)
    spread = lax.all_gather(renewed.astype(BF16), "rep", axis=1, tiled=True).astype(F32)[0]
    merged = (mixing * updated + (1.0 - mixing) * spread).astype(BF16)
    return (values[None], merged[None], renewed, momentum)


def solution(mesh):
    reps, shards = mesh.shape["rep"], mesh.shape["fsdp"]

    def on_device(*arrays):
        rows = arrays[5].shape[1]
        if shards == 4 and reps % 2 == 0 and reps > 2 and rows % STRIP == 0:
            return fused_call(reps, *arrays)
        return collective_form(*arrays)

    return jax.shard_map(
        on_device,
        mesh=mesh,
        in_specs=(P("rep", "fsdp", None),) * 5 + (P("fsdp", "rep", None),) * 2,
        out_specs=(P("rep", "fsdp", None),) * 2 + (P("fsdp", "rep", None),) * 2,
        check_vma=False,
    )
```

```python
import functools

import jax
import jax.numpy as jnp
from jax import lax
from jax.experimental import pallas as pl
from jax.experimental.pallas import tpu as pltpu
from jax.sharding import PartitionSpec as P

beta_one = 0.9
beta_two = 0.95
bias_one = 1.0 - 0.9**8
bias_two = 1.0 - 0.95**8
inner_rate = 0.25
decay_rate = 0.1
epsilon = 1e-08
outer_rate = 0.7
outer_mu = 0.9
mixing = 0.5

MESH = pl.DeviceIdType.MESH
BF16 = jnp.bfloat16
F32 = jnp.float32
CHUNKS = 4
AHEAD = 8
STRIP = 16


def inner_step(gradient, first, second, current):
    moment_new = beta_one * first + (1.0 - beta_one) * gradient
    second_new = beta_two * second + (1.0 - beta_two) * gradient * gradient
    stepped = moment_new / bias_one / (jnp.sqrt(second_new / bias_two) + epsilon)
    return current - inner_rate * (stepped + decay_rate * current)


def half_inner(raw, first, second, current, factor):
    scale = mixing * inner_rate / bias_one
    moment = (scale * beta_one) * first + (scale * (1.0 - beta_one) * factor) * raw
    second_new = (beta_two / bias_two) * second + ((1.0 - beta_two) * factor * factor / bias_two) * (raw * raw)
    return (mixing * (1.0 - inner_rate * decay_rate)) * current - moment / (jnp.sqrt(second_new) + epsilon)


def strips(rows, body, tall=STRIP):
    @pl.loop(0, rows // tall)
    def _(i):
        body(pl.multiple_of(i * tall, STRIP))


def fused(
    reps,
    hidden, upstream, weights, moment_one, moment_two, global_params, outer_momentum,
    val, mer, ren, mom,
    h_all, h_t, u_all, w, m1, m2, g, om,
    x_in, z_out, z_in, acc, spread, grad, p_own, p_far, p_out, p_in, y_out, y_in,
    local_sem,
    h_send, h_recv, u_send, u_recv, p_send, p_recv,
    x_send, x_recv, z_send, z_recv, gz_send, gz_recv, gx_send, gx_recv,
):
    tokens, width = hidden.shape[1:]
    block, columns = weights.shape[1:]
    rows = block // reps
    layers = reps // 2
    wide = columns // CHUNKS
    factor = float(width) ** (-0.5)

    me_rep = lax.axis_index("rep")
    me_shard = lax.axis_index("fsdp")
    z, x = me_rep // 2, me_rep % 2
    y, core = me_shard // 2, me_shard % 2
    sibling = y * 2 + (1 - core)
    across = (1 - y) * 2 + core
    diagonal = (1 - y) * 2 + (1 - core)
    shards = (me_shard, sibling, across, diagonal)
    x_peer = z * 2 + (1 - x)

    def layer(d):
        return (z + d + layers) % layers

    def at_shard(p):
        return (me_rep, p)

    def at_rep(r):
        return (r, me_shard)

    def row_block(owner):
        return pl.ds(pl.multiple_of(owner * rows, STRIP), rows)

    def cols(h):
        return pl.ds(h * wide, wide)

    def toks(j):
        return pl.ds(j * tokens, tokens)

    def remote(src, dst, send, recv, device):
        return pltpu.make_async_remote_copy(
            src_ref=src, dst_ref=dst, send_sem=send, recv_sem=recv,
            device_id=device, device_id_type=MESH,
        )

    loads = [
        (hidden.at[0, :, pl.ds(pl.multiple_of(me_shard * block, 128), block)], h_all.at[toks(0)]),
        (weights.at[0], w),
        (upstream.at[0], u_all.at[toks(0)]),
        (global_params.at[0], g),
        (outer_momentum.at[0], om),
        (moment_one.at[0], m1),
        (moment_two.at[0], m2),
    ]
    loads = [pltpu.make_async_copy(a, b, local_sem.at[i]) for i, (a, b) in enumerate(loads)]
    for copy in loads:
        copy.start()

    barrier = pltpu.get_barrier_semaphore()
    greeted = [at_shard(p) for p in shards[1:]] + [at_rep(x_peer)]
    greeted += [at_rep(layer(d) * 2 + x) for d in range(1, layers)]
    for device in greeted:
        pl.semaphore_signal(barrier, inc=1, device_id=device, device_id_type=MESH)
    pl.semaphore_wait(barrier, len(greeted))

    sent = []

    def go(copy):
        copy.start()
        sent.append(copy)

    def send_hidden(j):
        part = hidden.at[0, :, pl.ds(pl.multiple_of(shards[j] * block, 128), block)]
        go(remote(part, h_all.at[toks(j)], h_send.at[j - 1], h_recv.at[j - 1], at_shard(shards[j])))

    def hidden_in(j):
        dst = h_all.at[toks(j)]
        remote(dst, dst, h_send.at[j - 1], h_recv.at[j - 1], at_shard(shards[j])).wait_recv()

    def send_upstream(j, h):
        go(remote(
            upstream.at[0, :, cols(h)], u_all.at[toks(j), cols(h)],
            u_send.at[j - 1, h], u_recv.at[j - 1, h], at_shard(shards[j]),
        ))

    def upstream_in(j, h):
        dst = u_all.at[toks(j), cols(h)]
        remote(dst, dst, u_send.at[j - 1, h], u_recv.at[j - 1, h], at_shard(shards[j])).wait_recv()

    def pass_upstream(h):
        upstream_in(2, h)
        go(remote(
            u_all.at[toks(2), cols(h)], u_all.at[toks(3), cols(h)],
            u_send.at[2, h], u_recv.at[2, h], at_shard(sibling),
        ))

    order = tuple(range(1, layers)) + (0,)
    pieces = [(h, d) for h in range(CHUNKS) for d in order]

    def send_piece(h, d):
        part = weights.at[0, row_block(layer(d) * 2 + (1 - x)), cols(h)]
        go(remote(part, x_in.at[d, :, cols(h)], x_send.at[h, d], x_recv.at[h, d], at_rep(x_peer)))

    for piece in pieces[:AHEAD]:
        send_piece(*piece)
    send_hidden(3)
    send_hidden(2)
    send_hidden(1)
    for h in range(CHUNKS):
        send_upstream(1, h)

    def project(j, dst):
        @pl.loop(0, columns // 256)
        def _(n):
            at = pl.ds(pl.multiple_of(n * 256, 256), 256)
            dst[:, at] = jnp.dot(h_all[toks(j), :], w[:, at], preferred_element_type=F32)

    def turn(j):
        @pl.loop(0, block // 128)
        def _(i):
            at = pl.ds(pl.multiple_of(i * 128, 128), 128)
            h_t[at, toks(j)] = h_all[toks(j), at].T

    loads[0].wait()
    loads[1].wait()
    project(0, p_own)
    turn(0)
    hidden_in(1)
    project(1, p_out.at[0])
    go(remote(p_out.at[0], p_in.at[0], p_send.at[0], p_recv.at[0], at_shard(sibling)))
    turn(1)

    tall = rows // 3 if rows % 48 == 0 else STRIP

    def pairs(h):
        for d in order:
            dst = x_in.at[d, :, cols(h)]
            remote(dst, dst, x_send.at[h, d], x_recv.at[h, d], at_rep(x_peer)).wait_recv()
            later = h * layers + order.index(d) + AHEAD
            if later < len(pieces):
                send_piece(*pieces[later])
            base = (layer(d) * 2 + x) * rows

            def pair(i, d=d, base=base):
                here = pl.ds(pl.multiple_of(base + i, STRIP), tall)
                total = w[here, cols(h)].astype(F32) + x_in[d, pl.ds(i, tall), cols(h)].astype(F32)
                if d == 0:
                    acc[pl.ds(i, tall), cols(h)] = total
                else:
                    z_out[d - 1, pl.ds(i, tall), cols(h)] = total.astype(BF16)

            strips(rows, pair, tall)
            if d:
                go(remote(
                    z_out.at[d - 1, :, cols(h)], z_in.at[d - 1, :, cols(h)],
                    z_send.at[h, d - 1], z_recv.at[h, d - 1], at_rep(layer(d) * 2 + x),
                ))

    def renew(h):
        for d in range(1, layers):
            dst = z_in.at[d - 1, :, cols(h)]
            remote(dst, dst, z_send.at[h, d - 1], z_recv.at[h, d - 1], at_rep(me_rep)).wait_recv()

        def outer(i):
            here = pl.ds(i, tall)
            summed = acc[here, cols(h)]
            for d in range(1, layers):
                summed = summed + z_in[d - 1, here, cols(h)].astype(F32)
            now = g[here, cols(h)]
            pseudo = now - summed / reps
            momentum = outer_mu * om[here, cols(h)] + pseudo
            renewed = now - outer_rate * (pseudo + outer_mu * momentum)
            mom[here, cols(h)] = momentum
            ren[here, cols(h)] = renewed
            at = pl.ds(pl.multiple_of(me_rep * rows + i, STRIP), tall)
            spread[at, cols(h)] = renewed.astype(BF16)

        strips(rows, outer, tall)
        own = spread.at[row_block(me_rep), cols(h)]
        for d in order[:-1]:
            go(remote(own, own, gz_send.at[h, d - 1], gz_recv.at[h, d - 1], at_rep(layer(d) * 2 + x)))
        go(remote(own, own, gx_send.at[h, 0], gx_recv.at[h, 0], at_rep(x_peer)))

    near_first = (1,) + tuple(range(layers - 1, 1, -1))

    def forward(h):
        for d in near_first:
            part = spread.at[row_block(layer(-d) * 2 + x), cols(h)]
            remote(part, part, gz_send.at[h, d - 1], gz_recv.at[h, d - 1], at_rep(me_rep)).wait_recv()
            go(remote(part, part, gx_send.at[h, d], gx_recv.at[h, d], at_rep(x_peer)))

    part_rows = block // 3
    high = 48 if block % 48 == 0 else STRIP

    def inner(h):
        upstream_in(1, h)
        upstream_in(3, h)

        @pl.loop(0, 3)
        def _(part):
            at = pl.ds(pl.multiple_of(part * part_rows, STRIP), part_rows)
            grad[at, cols(h)] = jnp.dot(h_t[at, :], u_all[:, cols(h)], preferred_element_type=F32)

        def step(i):
            here = (pl.ds(i, high), cols(h))
            grad[here] = half_inner(
                grad[here], m1[here].astype(F32), m2[here].astype(F32), w[here].astype(F32), factor
            )

        strips(block, step, high)

    loads[3].wait()
    loads[4].wait()
    pairs(0)
    pairs(1)
    renew(0)
    send_upstream(2, 0)
    pairs(2)
    renew(1)
    send_upstream(2, 1)
    pairs(3)
    renew(2)
    forward(0)
    send_upstream(2, 2)
    send_upstream(2, 3)
    renew(3)
    forward(1)

    hidden_in(3)
    project(3, p_out.at[1])
    go(remote(p_out.at[1], p_in.at[1], p_send.at[1], p_recv.at[1], at_shard(sibling)))
    hidden_in(2)
    project(2, p_far)
    remote(p_in.at[1], p_in.at[1], p_send.at[1], p_recv.at[1], at_shard(sibling)).wait_recv()

    def chip_sum(i):
        here = pl.ds(i, STRIP)
        y_out[here, :] = (p_far[here, :] + p_in[1, here, :]).astype(BF16)

    strips(tokens, chip_sum)
    go(remote(y_out, y_in, p_send.at[2], p_recv.at[2], at_shard(across)))
    forward(2)
    turn(3)
    turn(2)
    loads[2].wait()
    loads[5].wait()
    loads[6].wait()
    pass_upstream(0)
    pass_upstream(1)
    inner(0)
    forward(3)
    pass_upstream(2)
    inner(1)
    pass_upstream(3)
    inner(2)
    inner(3)

    remote(p_in.at[0], p_in.at[0], p_send.at[0], p_recv.at[0], at_shard(sibling)).wait_recv()
    remote(y_in, y_in, p_send.at[2], p_recv.at[2], at_shard(across)).wait_recv()

    def finish(i):
        here = pl.ds(i, STRIP)
        total = p_own[here, :] + p_in[0, here, :] + y_in[here, :].astype(F32)
        val[here, :] = (total * factor).astype(BF16)

    strips(tokens, finish)

    def merge(owner):
        base = owner * rows

        def body(i):
            here = pl.ds(pl.multiple_of(base + i, STRIP), STRIP)
            mer[here, :] = (grad[here, :] + (1.0 - mixing) * spread[here, :].astype(F32)).astype(BF16)

        strips(rows, body)

    merge(me_rep)
    for d in near_first:
        merge(layer(-d) * 2 + x)
    for d in (0,) + near_first:
        owner = layer(-d) * 2 + (1 - x)
        for h in range(CHUNKS):
            part = spread.at[row_block(owner), cols(h)]
            remote(part, part, gx_send.at[h, d], gx_recv.at[h, d], at_rep(x_peer)).wait_recv()
        merge(owner)

    for copy in sent:
        copy.wait_send()


def fused_call(reps, hidden, upstream, weights, moment_one, moment_two, global_params, outer_momentum):
    tokens = hidden.shape[1]
    block, columns = weights.shape[1:]
    rows = block // reps
    layers = reps // 2
    dma = pltpu.SemaphoreType.DMA
    scratch = [
        pltpu.VMEM((4 * tokens, block), BF16),
        pltpu.VMEM((block, 4 * tokens), BF16),
        pltpu.VMEM((4 * tokens, columns), BF16),
        pltpu.VMEM((block, columns), BF16),
        pltpu.VMEM((block, columns), BF16),
        pltpu.VMEM((block, columns), BF16),
        pltpu.VMEM((rows, columns), F32),
        pltpu.VMEM((rows, columns), F32),
        pltpu.VMEM((layers, rows, columns), BF16),
        pltpu.VMEM((layers - 1, rows, columns), BF16),
        pltpu.VMEM((layers - 1, rows, columns), BF16),
        pltpu.VMEM((rows, columns), F32),
        pltpu.VMEM((block, columns), BF16),
        pltpu.VMEM((block, columns), F32),
        pltpu.VMEM((tokens, columns), F32),
        pltpu.VMEM((tokens, columns), F32),
        pltpu.VMEM((2, tokens, columns), F32),
        pltpu.VMEM((2, tokens, columns), F32),
        pltpu.VMEM((tokens, columns), BF16),
        pltpu.VMEM((tokens, columns), BF16),
        dma((7,)),
        dma((3,)), dma((3,)), dma((3, CHUNKS)), dma((3, CHUNKS)), dma((3,)), dma((3,)),
        dma((CHUNKS, layers)), dma((CHUNKS, layers)),
        dma((CHUNKS, layers - 1)), dma((CHUNKS, layers - 1)),
        dma((CHUNKS, layers - 1)), dma((CHUNKS, layers - 1)),
        dma((CHUNKS, layers)), dma((CHUNKS, layers)),
    ]
    anywhere = pl.BlockSpec(memory_space=pl.ANY)
    results = pl.pallas_call(
        functools.partial(fused, reps),
        out_shape=(
            pltpu.VMEM((tokens, columns), BF16),
            pltpu.VMEM((block, columns), BF16),
            pltpu.VMEM((rows, columns), F32),
            pltpu.VMEM((rows, columns), F32),
        ),
        in_specs=[anywhere] * 7,
        out_specs=[pl.BlockSpec(memory_space=pltpu.VMEM)] * 4,
        scratch_shapes=scratch,
        compiler_params=pltpu.CompilerParams(
            collective_id=0, has_side_effects=True, vmem_limit_bytes=59 * 1024 * 1024
        ),
        cost_estimate=pl.CostEstimate(
            flops=4 * tokens * hidden.shape[2] * columns, bytes_accessed=18 * 1024 * 1024, transcendentals=0
        ),
    )(hidden, upstream, weights, moment_one, moment_two, global_params, outer_momentum)
    return pl.pallas_call(
        write_out,
        out_shape=tuple(jax.ShapeDtypeStruct((1,) + a.shape, a.dtype) for a in results),
        in_specs=[pl.BlockSpec(memory_space=pltpu.VMEM)] * 4,
        out_specs=[anywhere] * 4,
        scratch_shapes=[dma((4,))],
        compiler_params=pltpu.CompilerParams(vmem_limit_bytes=8 * 1024 * 1024),
        cost_estimate=pl.CostEstimate(flops=0, bytes_accessed=8 * 1024 * 1024, transcendentals=0),
    )(*results)


def write_out(*refs):
    sources, targets, done = refs[:4], refs[4:8], refs[8]
    copies = [
        pltpu.make_async_copy(a, b.at[0], done.at[i]) for i, (a, b) in enumerate(zip(sources, targets))
    ]
    for copy in copies:
        copy.start()
    for copy in copies:
        copy.wait()


def collective_form(hidden, upstream, weights, moment_one, moment_two, global_params, outer_momentum):
    factor = float(hidden.shape[2]) ** (-0.5)
    tokens, grads_in = hidden[0], upstream[0]
    gathered = lax.all_gather(weights, "fsdp", axis=1, tiled=True)[0]
    values = (jnp.dot(tokens, gathered, preferred_element_type=F32) * factor).astype(BF16)
    partial = lax.dot_general(tokens, grads_in, (((0,), (0,)), ((), ())), preferred_element_type=F32)
    gradient = lax.psum_scatter(
        (partial * factor).astype(BF16), "fsdp", scatter_dimension=0, tiled=True
    ).astype(F32)
    updated = inner_step(
        gradient, moment_one[0].astype(F32), moment_two[0].astype(F32), weights[0].astype(F32)
    )
    owned = lax.psum_scatter(weights.astype(F32), "rep", scatter_dimension=1, tiled=True)
    pseudo = global_params - owned / lax.axis_size("rep")
    momentum = outer_mu * outer_momentum + pseudo
    renewed = global_params - outer_rate * (pseudo + outer_mu * momentum)
    spread = lax.all_gather(renewed.astype(BF16), "rep", axis=1, tiled=True).astype(F32)[0]
    merged = (mixing * updated + (1.0 - mixing) * spread).astype(BF16)
    return (values[None], merged[None], renewed, momentum)


def solution(mesh):
    reps, shards = mesh.shape["rep"], mesh.shape["fsdp"]

    def on_device(*arrays):
        rows = arrays[5].shape[1]
        if shards == 4 and reps % 2 == 0 and reps > 2 and rows % STRIP == 0:
            return fused_call(reps, *arrays)
        return collective_form(*arrays)

    return jax.shard_map(
        on_device,
        mesh=mesh,
        in_specs=(P("rep", "fsdp", None),) * 5 + (P("fsdp", "rep", None),) * 2,
        out_specs=(P("rep", "fsdp", None),) * 2 + (P("fsdp", "rep", None),) * 2,
        check_vma=False,
    )
```

```python
import functools

import jax
import jax.numpy as jnp
from jax import lax
from jax.experimental import pallas as pl
from jax.experimental.pallas import tpu as pltpu
from jax.sharding import PartitionSpec as P

beta_one = 0.9
beta_two = 0.95
bias_one = 1.0 - 0.9**8
bias_two = 1.0 - 0.95**8
inner_rate = 0.25
decay_rate = 0.1
epsilon = 1e-08
outer_rate = 0.7
outer_mu = 0.9
mixing = 0.5

MESH = pl.DeviceIdType.MESH
BF16 = jnp.bfloat16
F32 = jnp.float32
CHUNKS = 3
UP_CHUNKS = 2
AHEAD = 8
STRIP = 16


def inner_step(gradient, first, second, current):
    moment_new = beta_one * first + (1.0 - beta_one) * gradient
    second_new = beta_two * second + (1.0 - beta_two) * gradient * gradient
    stepped = moment_new / bias_one / (jnp.sqrt(second_new / bias_two) + epsilon)
    return current - inner_rate * (stepped + decay_rate * current)


def half_inner(raw, first, second, current, factor):
    scale = mixing * inner_rate / bias_one
    moment = (scale * beta_one) * first + (scale * (1.0 - beta_one) * factor) * raw
    second_new = (beta_two / bias_two) * second + ((1.0 - beta_two) * factor * factor / bias_two) * (raw * raw)
    return (mixing * (1.0 - inner_rate * decay_rate)) * current - moment / (jnp.sqrt(second_new) + epsilon)


def strips(rows, body, tall=STRIP):
    @pl.loop(0, rows // tall)
    def _(i):
        body(pl.multiple_of(i * tall, STRIP))


def fused(
    reps,
    hidden, upstream, weights, moment_one, moment_two, global_params, outer_momentum,
    val, mer, ren, mom,
    h_all, h_t, u_all, w, m1, m2, g, om,
    x_in, z_out, z_in, acc, spread, grad, p_own, p_far, p_out, p_in, y_out, y_in,
    local_sem,
    h_send, h_recv, u_send, u_recv, p_send, p_recv,
    x_send, x_recv, z_send, z_recv, gz_send, gz_recv, gx_send, gx_recv,
):
    tokens, width = hidden.shape[1:]
    block, columns = weights.shape[1:]
    rows = block // reps
    layers = reps // 2
    wide = columns // UP_CHUNKS
    short = rows // CHUNKS
    factor = float(width) ** (-0.5)

    me_rep = lax.axis_index("rep")
    me_shard = lax.axis_index("fsdp")
    z, x = me_rep // 2, me_rep % 2
    y, core = me_shard // 2, me_shard % 2
    sibling = y * 2 + (1 - core)
    across = (1 - y) * 2 + core
    diagonal = (1 - y) * 2 + (1 - core)
    shards = (me_shard, sibling, across, diagonal)
    x_peer = z * 2 + (1 - x)

    def layer(d):
        return (z + d + layers) % layers

    def at_shard(p):
        return (me_rep, p)

    def at_rep(r):
        return (r, me_shard)

    def piece_of(owner, h):
        return pl.ds(pl.multiple_of(owner * rows + h * short, STRIP), short)

    def sub(h):
        return pl.ds(h * short, short)

    def cols(h):
        return pl.ds(h * wide, wide)

    def toks(j):
        return pl.ds(j * tokens, tokens)

    def remote(src, dst, send, recv, device):
        return pltpu.make_async_remote_copy(
            src_ref=src, dst_ref=dst, send_sem=send, recv_sem=recv,
            device_id=device, device_id_type=MESH,
        )

    loads = [
        (hidden.at[0, :, pl.ds(pl.multiple_of(me_shard * block, 128), block)], h_all.at[toks(0)]),
        (weights.at[0], w),
        (upstream.at[0], u_all.at[toks(0)]),
        (global_params.at[0], g),
        (outer_momentum.at[0], om),
        (moment_one.at[0], m1),
        (moment_two.at[0], m2),
    ]
    loads = [pltpu.make_async_copy(a, b, local_sem.at[i]) for i, (a, b) in enumerate(loads)]
    for copy in loads:
        copy.start()

    barrier = pltpu.get_barrier_semaphore()
    greeted = [at_shard(p) for p in shards[1:]] + [at_rep(x_peer)]
    greeted += [at_rep(layer(d) * 2 + x) for d in range(1, layers)]
    for device in greeted:
        pl.semaphore_signal(barrier, inc=1, device_id=device, device_id_type=MESH)
    pl.semaphore_wait(barrier, len(greeted))

    sent = []

    def go(copy):
        copy.start()
        sent.append(copy)

    def send_hidden(j):
        part = hidden.at[0, :, pl.ds(pl.multiple_of(shards[j] * block, 128), block)]
        go(remote(part, h_all.at[toks(j)], h_send.at[j - 1], h_recv.at[j - 1], at_shard(shards[j])))

    def hidden_in(j):
        dst = h_all.at[toks(j)]
        remote(dst, dst, h_send.at[j - 1], h_recv.at[j - 1], at_shard(shards[j])).wait_recv()

    def send_upstream(j, h):
        go(remote(
            upstream.at[0, :, cols(h)], u_all.at[toks(j), cols(h)],
            u_send.at[j - 1, h], u_recv.at[j - 1, h], at_shard(shards[j]),
        ))

    def upstream_in(j, h):
        dst = u_all.at[toks(j), cols(h)]
        remote(dst, dst, u_send.at[j - 1, h], u_recv.at[j - 1, h], at_shard(shards[j])).wait_recv()

    def pass_upstream(h):
        upstream_in(2, h)
        go(remote(
            u_all.at[toks(2), cols(h)], u_all.at[toks(3), cols(h)],
            u_send.at[2, h], u_recv.at[2, h], at_shard(sibling),
        ))

    order = tuple(range(1, layers)) + (0,)
    pieces = [(h, d) for h in range(CHUNKS) for d in order]

    def send_piece(h, d):
        part = weights.at[0, piece_of(layer(d) * 2 + (1 - x), h)]
        go(remote(part, x_in.at[d, sub(h)], x_send.at[h, d], x_recv.at[h, d], at_rep(x_peer)))

    for piece in pieces[:AHEAD]:
        send_piece(*piece)
    send_hidden(3)
    send_hidden(2)
    send_hidden(1)
    for h in range(UP_CHUNKS):
        send_upstream(1, h)

    def project(j, dst):
        @pl.loop(0, columns // 256)
        def _(n):
            at = pl.ds(pl.multiple_of(n * 256, 256), 256)
            dst[:, at] = jnp.dot(h_all[toks(j), :], w[:, at], preferred_element_type=F32)

    def turn(j):
        @pl.loop(0, block // 128)
        def _(i):
            at = pl.ds(pl.multiple_of(i * 128, 128), 128)
            h_t[at, toks(j)] = h_all[toks(j), at].T

    loads[0].wait()
    loads[1].wait()
    project(0, p_own)
    turn(0)
    hidden_in(1)
    project(1, p_out.at[0])
    go(remote(p_out.at[0], p_in.at[0], p_send.at[0], p_recv.at[0], at_shard(sibling)))
    turn(1)

    def pairs(h):
        for d in order:
            dst = x_in.at[d, sub(h)]
            remote(dst, dst, x_send.at[h, d], x_recv.at[h, d], at_rep(x_peer)).wait_recv()
            later = h * layers + order.index(d) + AHEAD
            if later < len(pieces):
                send_piece(*pieces[later])
            base = (layer(d) * 2 + x) * rows + h * short

            def pair(i, d=d, base=base):
                here = pl.ds(pl.multiple_of(base + i, STRIP), STRIP)
                mine = pl.ds(pl.multiple_of(h * short + i, STRIP), STRIP)
                total = w[here, :].astype(F32) + x_in[d, mine, :].astype(F32)
                if d == 0:
                    acc[mine, :] = total
                else:
                    z_out[d - 1, mine, :] = total.astype(BF16)

            strips(short, pair)
            if d:
                go(remote(
                    z_out.at[d - 1, sub(h)], z_in.at[d - 1, sub(h)],
                    z_send.at[h, d - 1], z_recv.at[h, d - 1], at_rep(layer(d) * 2 + x),
                ))

    def renew(h):
        for d in range(1, layers):
            dst = z_in.at[d - 1, sub(h)]
            remote(dst, dst, z_send.at[h, d - 1], z_recv.at[h, d - 1], at_rep(me_rep)).wait_recv()

        def outer(i):
            here = pl.ds(pl.multiple_of(h * short + i, STRIP), STRIP)
            summed = acc[here, :]
            for d in range(1, layers):
                summed = summed + z_in[d - 1, here, :].astype(F32)
            now = g[here, :]
            pseudo = now - summed / reps
            momentum = outer_mu * om[here, :] + pseudo
            renewed = now - outer_rate * (pseudo + outer_mu * momentum)
            mom[here, :] = momentum
            ren[here, :] = renewed
            at = pl.ds(pl.multiple_of(me_rep * rows + h * short + i, STRIP), STRIP)
            spread[at, :] = renewed.astype(BF16)

        strips(short, outer)
        own = spread.at[piece_of(me_rep, h)]
        for d in order[:-1]:
            go(remote(own, own, gz_send.at[h, d - 1], gz_recv.at[h, d - 1], at_rep(layer(d) * 2 + x)))
        go(remote(own, own, gx_send.at[h, 0], gx_recv.at[h, 0], at_rep(x_peer)))

    near_first = (1,) + tuple(range(layers - 1, 1, -1))

    def forward(h):
        for d in near_first:
            part = spread.at[piece_of(layer(-d) * 2 + x, h)]
            remote(part, part, gz_send.at[h, d - 1], gz_recv.at[h, d - 1], at_rep(me_rep)).wait_recv()
            go(remote(part, part, gx_send.at[h, d], gx_recv.at[h, d], at_rep(x_peer)))

    part_rows = block // 3
    high = STRIP

    def inner(h):
        upstream_in(1, h)
        upstream_in(3, h)

        @pl.loop(0, 3)
        def _(part):
            at = pl.ds(pl.multiple_of(part * part_rows, STRIP), part_rows)
            grad[at, cols(h)] = jnp.dot(h_t[at, :], u_all[:, cols(h)], preferred_element_type=F32)

        def step(i):
            here = (pl.ds(i, high), cols(h))
            grad[here] = half_inner(
                grad[here], m1[here].astype(F32), m2[here].astype(F32), w[here].astype(F32), factor
            )

        strips(block, step, high)

    loads[3].wait()
    loads[4].wait()
    pairs(0)
    pairs(1)
    renew(0)
    send_upstream(2, 0)
    pairs(2)
    renew(1)
    forward(0)
    send_upstream(2, 1)
    renew(2)
    forward(1)

    hidden_in(3)
    project(3, p_out.at[1])
    go(remote(p_out.at[1], p_in.at[1], p_send.at[1], p_recv.at[1], at_shard(sibling)))
    hidden_in(2)
    project(2, p_far)
    remote(p_in.at[1], p_in.at[1], p_send.at[1], p_recv.at[1], at_shard(sibling)).wait_recv()

    def chip_sum(i):
        here = pl.ds(i, STRIP)
        y_out[here, :] = (p_far[here, :] + p_in[1, here, :]).astype(BF16)

    strips(tokens, chip_sum)
    go(remote(y_out, y_in, p_send.at[2], p_recv.at[2], at_shard(across)))
    forward(2)
    turn(3)
    turn(2)
    loads[2].wait()
    loads[5].wait()
    loads[6].wait()
    pass_upstream(0)
    pass_upstream(1)
    inner(0)
    inner(1)

    remote(p_in.at[0], p_in.at[0], p_send.at[0], p_recv.at[0], at_shard(sibling)).wait_recv()
    remote(y_in, y_in, p_send.at[2], p_recv.at[2], at_shard(across)).wait_recv()

    def finish(i):
        here = pl.ds(i, STRIP)
        total = p_own[here, :] + p_in[0, here, :] + y_in[here, :].astype(F32)
        val[here, :] = (total * factor).astype(BF16)

    strips(tokens, finish)

    def merge(owner):
        base = owner * rows

        def body(i):
            here = pl.ds(pl.multiple_of(base + i, STRIP), STRIP)
            mer[here, :] = (grad[here, :] + (1.0 - mixing) * spread[here, :].astype(F32)).astype(BF16)

        strips(rows, body)

    merge(me_rep)
    for d in near_first:
        merge(layer(-d) * 2 + x)
    for d in (0,) + near_first:
        owner = layer(-d) * 2 + (1 - x)
        for h in range(CHUNKS):
            part = spread.at[piece_of(owner, h)]
            remote(part, part, gx_send.at[h, d], gx_recv.at[h, d], at_rep(x_peer)).wait_recv()
        merge(owner)

    for copy in sent:
        copy.wait_send()


def fused_call(reps, hidden, upstream, weights, moment_one, moment_two, global_params, outer_momentum):
    tokens = hidden.shape[1]
    block, columns = weights.shape[1:]
    rows = block // reps
    layers = reps // 2
    dma = pltpu.SemaphoreType.DMA
    scratch = [
        pltpu.VMEM((4 * tokens, block), BF16),
        pltpu.VMEM((block, 4 * tokens), BF16),
        pltpu.VMEM((4 * tokens, columns), BF16),
        pltpu.VMEM((block, columns), BF16),
        pltpu.VMEM((block, columns), BF16),
        pltpu.VMEM((block, columns), BF16),
        pltpu.VMEM((rows, columns), F32),
        pltpu.VMEM((rows, columns), F32),
        pltpu.VMEM((layers, rows, columns), BF16),
        pltpu.VMEM((layers - 1, rows, columns), BF16),
        pltpu.VMEM((layers - 1, rows, columns), BF16),
        pltpu.VMEM((rows, columns), F32),
        pltpu.VMEM((block, columns), BF16),
        pltpu.VMEM((block, columns), F32),
        pltpu.VMEM((tokens, columns), F32),
        pltpu.VMEM((tokens, columns), F32),
        pltpu.VMEM((2, tokens, columns), F32),
        pltpu.VMEM((2, tokens, columns), F32),
        pltpu.VMEM((tokens, columns), BF16),
        pltpu.VMEM((tokens, columns), BF16),
        dma((7,)),
        dma((3,)), dma((3,)), dma((3, UP_CHUNKS)), dma((3, UP_CHUNKS)), dma((3,)), dma((3,)),
        dma((CHUNKS, layers)), dma((CHUNKS, layers)),
        dma((CHUNKS, layers - 1)), dma((CHUNKS, layers - 1)),
        dma((CHUNKS, layers - 1)), dma((CHUNKS, layers - 1)),
        dma((CHUNKS, layers)), dma((CHUNKS, layers)),
    ]
    anywhere = pl.BlockSpec(memory_space=pl.ANY)
    results = pl.pallas_call(
        functools.partial(fused, reps),
        out_shape=(
            pltpu.VMEM((tokens, columns), BF16),
            pltpu.VMEM((block, columns), BF16),
            pltpu.VMEM((rows, columns), F32),
            pltpu.VMEM((rows, columns), F32),
        ),
        in_specs=[anywhere] * 7,
        out_specs=[pl.BlockSpec(memory_space=pltpu.VMEM)] * 4,
        scratch_shapes=scratch,
        compiler_params=pltpu.CompilerParams(
            collective_id=0, has_side_effects=True, vmem_limit_bytes=59 * 1024 * 1024
        ),
        cost_estimate=pl.CostEstimate(
            flops=4 * tokens * hidden.shape[2] * columns, bytes_accessed=18 * 1024 * 1024, transcendentals=0
        ),
    )(hidden, upstream, weights, moment_one, moment_two, global_params, outer_momentum)
    return pl.pallas_call(
        write_out,
        out_shape=tuple(jax.ShapeDtypeStruct((1,) + a.shape, a.dtype) for a in results),
        in_specs=[pl.BlockSpec(memory_space=pltpu.VMEM)] * 4,
        out_specs=[anywhere] * 4,
        scratch_shapes=[dma((4,))],
        compiler_params=pltpu.CompilerParams(vmem_limit_bytes=8 * 1024 * 1024),
        cost_estimate=pl.CostEstimate(flops=0, bytes_accessed=8 * 1024 * 1024, transcendentals=0),
    )(*results)


def write_out(*refs):
    sources, targets, done = refs[:4], refs[4:8], refs[8]
    copies = [
        pltpu.make_async_copy(a, b.at[0], done.at[i]) for i, (a, b) in enumerate(zip(sources, targets))
    ]
    for copy in copies:
        copy.start()
    for copy in copies:
        copy.wait()


def collective_form(hidden, upstream, weights, moment_one, moment_two, global_params, outer_momentum):
    factor = float(hidden.shape[2]) ** (-0.5)
    tokens, grads_in = hidden[0], upstream[0]
    gathered = lax.all_gather(weights, "fsdp", axis=1, tiled=True)[0]
    values = (jnp.dot(tokens, gathered, preferred_element_type=F32) * factor).astype(BF16)
    partial = lax.dot_general(tokens, grads_in, (((0,), (0,)), ((), ())), preferred_element_type=F32)
    gradient = lax.psum_scatter(
        (partial * factor).astype(BF16), "fsdp", scatter_dimension=0, tiled=True
    ).astype(F32)
    updated = inner_step(
        gradient, moment_one[0].astype(F32), moment_two[0].astype(F32), weights[0].astype(F32)
    )
    owned = lax.psum_scatter(weights.astype(F32), "rep", scatter_dimension=1, tiled=True)
    pseudo = global_params - owned / lax.axis_size("rep")
    momentum = outer_mu * outer_momentum + pseudo
    renewed = global_params - outer_rate * (pseudo + outer_mu * momentum)
    spread = lax.all_gather(renewed.astype(BF16), "rep", axis=1, tiled=True).astype(F32)[0]
    merged = (mixing * updated + (1.0 - mixing) * spread).astype(BF16)
    return (values[None], merged[None], renewed, momentum)


def solution(mesh):
    reps, shards = mesh.shape["rep"], mesh.shape["fsdp"]

    def on_device(*arrays):
        rows = arrays[5].shape[1]
        if shards == 4 and reps % 2 == 0 and reps > 2 and rows % (CHUNKS * STRIP) == 0:
            return fused_call(reps, *arrays)
        return collective_form(*arrays)

    return jax.shard_map(
        on_device,
        mesh=mesh,
        in_specs=(P("rep", "fsdp", None),) * 5 + (P("fsdp", "rep", None),) * 2,
        out_specs=(P("rep", "fsdp", None),) * 2 + (P("fsdp", "rep", None),) * 2,
        check_vma=False,
    )
```

```python
import functools

import jax
import jax.numpy as jnp
from jax import lax
from jax.experimental import pallas as pl
from jax.experimental.pallas import tpu as pltpu
from jax.sharding import PartitionSpec as P

beta_one = 0.9
beta_two = 0.95
bias_one = 1.0 - 0.9**8
bias_two = 1.0 - 0.95**8
inner_rate = 0.25
decay_rate = 0.1
epsilon = 1e-08
outer_rate = 0.7
outer_mu = 0.9
mixing = 0.5

MESH = pl.DeviceIdType.MESH
BF16 = jnp.bfloat16
F32 = jnp.float32
CHUNKS = 4
AHEAD = 8
STRIP = 16


def inner_step(gradient, first, second, current):
    moment_new = beta_one * first + (1.0 - beta_one) * gradient
    second_new = beta_two * second + (1.0 - beta_two) * gradient * gradient
    stepped = moment_new / bias_one / (jnp.sqrt(second_new / bias_two) + epsilon)
    return current - inner_rate * (stepped + decay_rate * current)


def half_inner(raw, first, second, current, factor):
    scale = mixing * inner_rate / bias_one
    moment = (scale * beta_one) * first + (scale * (1.0 - beta_one) * factor) * raw
    second_new = (beta_two / bias_two) * second + ((1.0 - beta_two) * factor * factor / bias_two) * (raw * raw)
    return (mixing * (1.0 - inner_rate * decay_rate)) * current - moment / (jnp.sqrt(second_new) + epsilon)


def strips(rows, body, tall=STRIP):
    @pl.loop(0, rows // tall)
    def _(i):
        body(pl.multiple_of(i * tall, STRIP))


def fused(
    reps,
    hidden, upstream, weights, moment_one, moment_two, global_params, outer_momentum,
    val, mer, ren, mom,
    h_all, h_t, u_all, w, m1, m2, g, om,
    x_in, z_out, z_in, acc, spread, grad, p_own, p_far, p_out, p_in, y_out, y_in,
    local_sem,
    h_send, h_recv, u_send, u_recv, p_send, p_recv,
    x_send, x_recv, z_send, z_recv, gz_send, gz_recv, gx_send, gx_recv,
):
    tokens, width = hidden.shape[1:]
    block, columns = weights.shape[1:]
    rows = block // reps
    layers = reps // 2
    wide = columns // CHUNKS
    factor = float(width) ** (-0.5)

    me_rep = lax.axis_index("rep")
    me_shard = lax.axis_index("fsdp")
    z, x = me_rep // 2, me_rep % 2
    y, core = me_shard // 2, me_shard % 2
    sibling = y * 2 + (1 - core)
    across = (1 - y) * 2 + core
    diagonal = (1 - y) * 2 + (1 - core)
    shards = (me_shard, sibling, across, diagonal)
    x_peer = z * 2 + (1 - x)

    def layer(d):
        return (z + d + layers) % layers

    def at_shard(p):
        return (me_rep, p)

    def at_rep(r):
        return (r, me_shard)

    def row_block(owner):
        return pl.ds(pl.multiple_of(owner * rows, STRIP), rows)

    def cols(h):
        return pl.ds(h * wide, wide)

    def toks(j):
        return pl.ds(j * tokens, tokens)

    def remote(src, dst, send, recv, device):
        return pltpu.make_async_remote_copy(
            src_ref=src, dst_ref=dst, send_sem=send, recv_sem=recv,
            device_id=device, device_id_type=MESH,
        )

    loads = [
        (hidden.at[0, :, pl.ds(pl.multiple_of(me_shard * block, 128), block)], h_all.at[toks(0)]),
        (weights.at[0], w),
        (upstream.at[0], u_all.at[toks(0)]),
        (global_params.at[0], g),
        (outer_momentum.at[0], om),
        (moment_one.at[0], m1),
        (moment_two.at[0], m2),
    ]
    loads = [pltpu.make_async_copy(a, b, local_sem.at[i]) for i, (a, b) in enumerate(loads)]
    for copy in loads:
        copy.start()

    barrier = pltpu.get_barrier_semaphore()
    greeted = [at_shard(p) for p in shards[1:]] + [at_rep(x_peer)]
    greeted += [at_rep(layer(d) * 2 + x) for d in range(1, layers)]
    for device in greeted:
        pl.semaphore_signal(barrier, inc=1, device_id=device, device_id_type=MESH)
    pl.semaphore_wait(barrier, len(greeted))

    sent = []

    def go(copy):
        copy.start()
        sent.append(copy)

    def send_hidden(j):
        part = hidden.at[0, :, pl.ds(pl.multiple_of(shards[j] * block, 128), block)]
        go(remote(part, h_all.at[toks(j)], h_send.at[j - 1], h_recv.at[j - 1], at_shard(shards[j])))

    def hidden_in(j):
        dst = h_all.at[toks(j)]
        remote(dst, dst, h_send.at[j - 1], h_recv.at[j - 1], at_shard(shards[j])).wait_recv()

    def send_upstream(j, h):
        go(remote(
            upstream.at[0, :, cols(h)], u_all.at[toks(j), cols(h)],
            u_send.at[j - 1, h], u_recv.at[j - 1, h], at_shard(shards[j]),
        ))

    def upstream_in(j, h):
        dst = u_all.at[toks(j), cols(h)]
        remote(dst, dst, u_send.at[j - 1, h], u_recv.at[j - 1, h], at_shard(shards[j])).wait_recv()

    def pass_upstream(h):
        upstream_in(2, h)
        go(remote(
            u_all.at[toks(2), cols(h)], u_all.at[toks(3), cols(h)],
            u_send.at[2, h], u_recv.at[2, h], at_shard(sibling),
        ))

    order = tuple(range(1, layers)) + (0,)
    pieces = [(h, d) for h in range(CHUNKS) for d in order]

    def send_piece(h, d):
        part = weights.at[0, row_block(layer(d) * 2 + (1 - x)), cols(h)]
        go(remote(part, x_in.at[d, :, cols(h)], x_send.at[h, d], x_recv.at[h, d], at_rep(x_peer)))

    for piece in pieces[:AHEAD]:
        send_piece(*piece)
    send_hidden(3)
    send_hidden(2)
    for h in range(CHUNKS):
        send_upstream(2, h)
    send_hidden(1)
    for h in range(CHUNKS):
        send_upstream(1, h)

    def project(j, dst):
        @pl.loop(0, columns // 256)
        def _(n):
            at = pl.ds(pl.multiple_of(n * 256, 256), 256)
            dst[:, at] = jnp.dot(h_all[toks(j), :], w[:, at], preferred_element_type=F32)

    def turn(j):
        @pl.loop(0, block // 128)
        def _(i):
            at = pl.ds(pl.multiple_of(i * 128, 128), 128)
            h_t[at, toks(j)] = h_all[toks(j), at].T

    loads[0].wait()
    loads[1].wait()
    project(0, p_own)
    turn(0)
    hidden_in(1)
    project(1, p_out.at[0])
    go(remote(p_out.at[0], p_in.at[0], p_send.at[0], p_recv.at[0], at_shard(sibling)))
    turn(1)

    tall = rows // 3 if rows % 48 == 0 else STRIP

    def pairs(h):
        for d in order:
            dst = x_in.at[d, :, cols(h)]
            remote(dst, dst, x_send.at[h, d], x_recv.at[h, d], at_rep(x_peer)).wait_recv()
            later = h * layers + order.index(d) + AHEAD
            if later < len(pieces):
                send_piece(*pieces[later])
            base = (layer(d) * 2 + x) * rows

            def pair(i, d=d, base=base):
                here = pl.ds(pl.multiple_of(base + i, STRIP), tall)
                total = w[here, cols(h)].astype(F32) + x_in[d, pl.ds(i, tall), cols(h)].astype(F32)
                if d == 0:
                    acc[pl.ds(i, tall), cols(h)] = total
                else:
                    z_out[d - 1, pl.ds(i, tall), cols(h)] = total.astype(BF16)

            strips(rows, pair, tall)
            if d:
                go(remote(
                    z_out.at[d - 1, :, cols(h)], z_in.at[d - 1, :, cols(h)],
                    z_send.at[h, d - 1], z_recv.at[h, d - 1], at_rep(layer(d) * 2 + x),
                ))

    def renew(h):
        for d in range(1, layers):
            dst = z_in.at[d - 1, :, cols(h)]
            remote(dst, dst, z_send.at[h, d - 1], z_recv.at[h, d - 1], at_rep(me_rep)).wait_recv()

        def outer(i):
            here = pl.ds(i, tall)
            summed = acc[here, cols(h)]
            for d in range(1, layers):
                summed = summed + z_in[d - 1, here, cols(h)].astype(F32)
            now = g[here, cols(h)]
            pseudo = now - summed / reps
            momentum = outer_mu * om[here, cols(h)] + pseudo
            renewed = now - outer_rate * (pseudo + outer_mu * momentum)
            mom[here, cols(h)] = momentum
            ren[here, cols(h)] = renewed
            at = pl.ds(pl.multiple_of(me_rep * rows + i, STRIP), tall)
            spread[at, cols(h)] = renewed.astype(BF16)

        strips(rows, outer, tall)
        own = spread.at[row_block(me_rep), cols(h)]
        for d in order[:-1]:
            go(remote(own, own, gz_send.at[h, d - 1], gz_recv.at[h, d - 1], at_rep(layer(d) * 2 + x)))
        go(remote(own, own, gx_send.at[h, 0], gx_recv.at[h, 0], at_rep(x_peer)))

    near_first = (1,) + tuple(range(layers - 1, 1, -1))

    def forward(h):
        for d in near_first:
            part = spread.at[row_block(layer(-d) * 2 + x), cols(h)]
            remote(part, part, gz_send.at[h, d - 1], gz_recv.at[h, d - 1], at_rep(me_rep)).wait_recv()
            go(remote(part, part, gx_send.at[h, d], gx_recv.at[h, d], at_rep(x_peer)))

    part_rows = block // 3
    high = 48 if block % 48 == 0 else STRIP

    def inner(h):
        upstream_in(1, h)
        upstream_in(3, h)

        @pl.loop(0, 3)
        def _(part):
            at = pl.ds(pl.multiple_of(part * part_rows, STRIP), part_rows)
            grad[at, cols(h)] = jnp.dot(h_t[at, :], u_all[:, cols(h)], preferred_element_type=F32)

        def step(i):
            here = (pl.ds(i, high), cols(h))
            grad[here] = half_inner(
                grad[here], m1[here].astype(F32), m2[here].astype(F32), w[here].astype(F32), factor
            )

        strips(block, step, high)

    loads[3].wait()
    loads[4].wait()
    pairs(0)
    pairs(1)
    renew(0)
    pairs(2)
    renew(1)
    pairs(3)
    renew(2)
    forward(0)
    renew(3)
    forward(1)

    hidden_in(3)
    project(3, p_out.at[1])
    go(remote(p_out.at[1], p_in.at[1], p_send.at[1], p_recv.at[1], at_shard(sibling)))
    hidden_in(2)
    project(2, p_far)
    remote(p_in.at[1], p_in.at[1], p_send.at[1], p_recv.at[1], at_shard(sibling)).wait_recv()

    def chip_sum(i):
        here = pl.ds(i, STRIP)
        y_out[here, :] = (p_far[here, :] + p_in[1, here, :]).astype(BF16)

    strips(tokens, chip_sum)
    go(remote(y_out, y_in, p_send.at[2], p_recv.at[2], at_shard(across)))
    forward(2)
    turn(3)
    turn(2)
    loads[2].wait()
    loads[5].wait()
    loads[6].wait()
    pass_upstream(0)
    pass_upstream(1)
    inner(0)
    forward(3)
    pass_upstream(2)
    inner(1)
    pass_upstream(3)
    inner(2)
    inner(3)

    remote(p_in.at[0], p_in.at[0], p_send.at[0], p_recv.at[0], at_shard(sibling)).wait_recv()
    remote(y_in, y_in, p_send.at[2], p_recv.at[2], at_shard(across)).wait_recv()

    def finish(i):
        here = pl.ds(i, STRIP)
        total = p_own[here, :] + p_in[0, here, :] + y_in[here, :].astype(F32)
        val[here, :] = (total * factor).astype(BF16)

    strips(tokens, finish)

    def merge(owner):
        base = owner * rows

        def body(i):
            here = pl.ds(pl.multiple_of(base + i, STRIP), STRIP)
            mer[here, :] = (grad[here, :] + (1.0 - mixing) * spread[here, :].astype(F32)).astype(BF16)

        strips(rows, body)

    merge(me_rep)
    for d in near_first:
        merge(layer(-d) * 2 + x)
    for d in (0,) + near_first:
        owner = layer(-d) * 2 + (1 - x)
        for h in range(CHUNKS):
            part = spread.at[row_block(owner), cols(h)]
            remote(part, part, gx_send.at[h, d], gx_recv.at[h, d], at_rep(x_peer)).wait_recv()
        merge(owner)

    for copy in sent:
        copy.wait_send()


def fused_call(reps, hidden, upstream, weights, moment_one, moment_two, global_params, outer_momentum):
    tokens = hidden.shape[1]
    block, columns = weights.shape[1:]
    rows = block // reps
    layers = reps // 2
    dma = pltpu.SemaphoreType.DMA
    scratch = [
        pltpu.VMEM((4 * tokens, block), BF16),
        pltpu.VMEM((block, 4 * tokens), BF16),
        pltpu.VMEM((4 * tokens, columns), BF16),
        pltpu.VMEM((block, columns), BF16),
        pltpu.VMEM((block, columns), BF16),
        pltpu.VMEM((block, columns), BF16),
        pltpu.VMEM((rows, columns), F32),
        pltpu.VMEM((rows, columns), F32),
        pltpu.VMEM((layers, rows, columns), BF16),
        pltpu.VMEM((layers - 1, rows, columns), BF16),
        pltpu.VMEM((layers - 1, rows, columns), BF16),
        pltpu.VMEM((rows, columns), F32),
        pltpu.VMEM((block, columns), BF16),
        pltpu.VMEM((block, columns), F32),
        pltpu.VMEM((tokens, columns), F32),
        pltpu.VMEM((tokens, columns), F32),
        pltpu.VMEM((2, tokens, columns), F32),
        pltpu.VMEM((2, tokens, columns), F32),
        pltpu.VMEM((tokens, columns), BF16),
        pltpu.VMEM((tokens, columns), BF16),
        dma((7,)),
        dma((3,)), dma((3,)), dma((3, CHUNKS)), dma((3, CHUNKS)), dma((3,)), dma((3,)),
        dma((CHUNKS, layers)), dma((CHUNKS, layers)),
        dma((CHUNKS, layers - 1)), dma((CHUNKS, layers - 1)),
        dma((CHUNKS, layers - 1)), dma((CHUNKS, layers - 1)),
        dma((CHUNKS, layers)), dma((CHUNKS, layers)),
    ]
    anywhere = pl.BlockSpec(memory_space=pl.ANY)
    results = pl.pallas_call(
        functools.partial(fused, reps),
        out_shape=(
            pltpu.VMEM((tokens, columns), BF16),
            pltpu.VMEM((block, columns), BF16),
            pltpu.VMEM((rows, columns), F32),
            pltpu.VMEM((rows, columns), F32),
        ),
        in_specs=[anywhere] * 7,
        out_specs=[pl.BlockSpec(memory_space=pltpu.VMEM)] * 4,
        scratch_shapes=scratch,
        compiler_params=pltpu.CompilerParams(
            collective_id=0, has_side_effects=True, vmem_limit_bytes=59 * 1024 * 1024
        ),
        cost_estimate=pl.CostEstimate(
            flops=4 * tokens * hidden.shape[2] * columns, bytes_accessed=18 * 1024 * 1024, transcendentals=0
        ),
    )(hidden, upstream, weights, moment_one, moment_two, global_params, outer_momentum)
    return pl.pallas_call(
        write_out,
        out_shape=tuple(jax.ShapeDtypeStruct((1,) + a.shape, a.dtype) for a in results),
        in_specs=[pl.BlockSpec(memory_space=pltpu.VMEM)] * 4,
        out_specs=[anywhere] * 4,
        scratch_shapes=[dma((4,))],
        compiler_params=pltpu.CompilerParams(vmem_limit_bytes=8 * 1024 * 1024),
        cost_estimate=pl.CostEstimate(flops=0, bytes_accessed=8 * 1024 * 1024, transcendentals=0),
    )(*results)


def write_out(*refs):
    sources, targets, done = refs[:4], refs[4:8], refs[8]
    copies = [
        pltpu.make_async_copy(a, b.at[0], done.at[i]) for i, (a, b) in enumerate(zip(sources, targets))
    ]
    for copy in copies:
        copy.start()
    for copy in copies:
        copy.wait()


def collective_form(hidden, upstream, weights, moment_one, moment_two, global_params, outer_momentum):
    factor = float(hidden.shape[2]) ** (-0.5)
    tokens, grads_in = hidden[0], upstream[0]
    gathered = lax.all_gather(weights, "fsdp", axis=1, tiled=True)[0]
    values = (jnp.dot(tokens, gathered, preferred_element_type=F32) * factor).astype(BF16)
    partial = lax.dot_general(tokens, grads_in, (((0,), (0,)), ((), ())), preferred_element_type=F32)
    gradient = lax.psum_scatter(
        (partial * factor).astype(BF16), "fsdp", scatter_dimension=0, tiled=True
    ).astype(F32)
    updated = inner_step(
        gradient, moment_one[0].astype(F32), moment_two[0].astype(F32), weights[0].astype(F32)
    )
    owned = lax.psum_scatter(weights.astype(F32), "rep", scatter_dimension=1, tiled=True)
    pseudo = global_params - owned / lax.axis_size("rep")
    momentum = outer_mu * outer_momentum + pseudo
    renewed = global_params - outer_rate * (pseudo + outer_mu * momentum)
    spread = lax.all_gather(renewed.astype(BF16), "rep", axis=1, tiled=True).astype(F32)[0]
    merged = (mixing * updated + (1.0 - mixing) * spread).astype(BF16)
    return (values[None], merged[None], renewed, momentum)


def solution(mesh):
    reps, shards = mesh.shape["rep"], mesh.shape["fsdp"]

    def on_device(*arrays):
        rows = arrays[5].shape[1]
        if shards == 4 and reps % 2 == 0 and reps > 2 and rows % STRIP == 0:
            return fused_call(reps, *arrays)
        return collective_form(*arrays)

    return jax.shard_map(
        on_device,
        mesh=mesh,
        in_specs=(P("rep", "fsdp", None),) * 5 + (P("fsdp", "rep", None),) * 2,
        out_specs=(P("rep", "fsdp", None),) * 2 + (P("fsdp", "rep", None),) * 2,
        check_vma=False,
    )
```

```python
import functools

import jax
import jax.numpy as jnp
from jax import lax
from jax.experimental import pallas as pl
from jax.experimental.pallas import tpu as pltpu
from jax.sharding import PartitionSpec as P

beta_one = 0.9
beta_two = 0.95
bias_one = 1.0 - 0.9**8
bias_two = 1.0 - 0.95**8
inner_rate = 0.25
decay_rate = 0.1
epsilon = 1e-08
outer_rate = 0.7
outer_mu = 0.9
mixing = 0.5

MESH = pl.DeviceIdType.MESH
BF16 = jnp.bfloat16
F32 = jnp.float32
CHUNKS = 4
AHEAD = 8
STRIP = 16


def inner_step(gradient, first, second, current):
    moment_new = beta_one * first + (1.0 - beta_one) * gradient
    second_new = beta_two * second + (1.0 - beta_two) * gradient * gradient
    stepped = moment_new / bias_one / (jnp.sqrt(second_new / bias_two) + epsilon)
    return current - inner_rate * (stepped + decay_rate * current)


def half_inner(raw, first, second, current, factor):
    scale = mixing * inner_rate / bias_one
    moment = (scale * beta_one) * first + (scale * (1.0 - beta_one) * factor) * raw
    second_new = (beta_two / bias_two) * second + ((1.0 - beta_two) * factor * factor / bias_two) * (raw * raw)
    return (mixing * (1.0 - inner_rate * decay_rate)) * current - moment / (jnp.sqrt(second_new) + epsilon)


def strips(rows, body, tall=STRIP):
    @pl.loop(0, rows // tall)
    def _(i):
        body(pl.multiple_of(i * tall, STRIP))


def fused(
    reps,
    hidden, upstream, weights, moment_one, moment_two, global_params, outer_momentum,
    val, mer, ren, mom,
    h_all, h_t, u_all, w, m1, m2, g, om,
    x_in, z_out, z_in, acc, spread, grad, p_own, p_far, p_out, p_in, y_out, y_in,
    local_sem,
    h_send, h_recv, u_send, u_recv, p_send, p_recv,
    x_send, x_recv, z_send, z_recv, gz_send, gz_recv, gx_send, gx_recv,
):
    tokens, width = hidden.shape[1:]
    block, columns = weights.shape[1:]
    rows = block // reps
    layers = reps // 2
    wide = columns // CHUNKS
    factor = float(width) ** (-0.5)

    me_rep = lax.axis_index("rep")
    me_shard = lax.axis_index("fsdp")
    z, x = me_rep // 2, me_rep % 2
    y, core = me_shard // 2, me_shard % 2
    sibling = y * 2 + (1 - core)
    across = (1 - y) * 2 + core
    diagonal = (1 - y) * 2 + (1 - core)
    shards = (me_shard, sibling, across, diagonal)
    x_peer = z * 2 + (1 - x)

    def layer(d):
        return (z + d + layers) % layers

    def at_shard(p):
        return (me_rep, p)

    def at_rep(r):
        return (r, me_shard)

    def row_block(owner):
        return pl.ds(pl.multiple_of(owner * rows, STRIP), rows)

    def cols(h):
        return pl.ds(h * wide, wide)

    def toks(j):
        return pl.ds(j * tokens, tokens)

    def remote(src, dst, send, recv, device):
        return pltpu.make_async_remote_copy(
            src_ref=src, dst_ref=dst, send_sem=send, recv_sem=recv,
            device_id=device, device_id_type=MESH,
        )

    loads = [
        (hidden.at[0, :, pl.ds(pl.multiple_of(me_shard * block, 128), block)], h_all.at[toks(0)]),
        (weights.at[0], w),
        (upstream.at[0], u_all.at[toks(0)]),
        (global_params.at[0], g),
        (outer_momentum.at[0], om),
        (moment_one.at[0], m1),
        (moment_two.at[0], m2),
    ]
    loads = [pltpu.make_async_copy(a, b, local_sem.at[i]) for i, (a, b) in enumerate(loads)]
    for copy in loads:
        copy.start()

    barrier = pltpu.get_barrier_semaphore()
    greeted = [at_shard(p) for p in shards[1:]] + [at_rep(x_peer)]
    greeted += [at_rep(layer(d) * 2 + x) for d in range(1, layers)]
    for device in greeted:
        pl.semaphore_signal(barrier, inc=1, device_id=device, device_id_type=MESH)
    pl.semaphore_wait(barrier, len(greeted))

    sent = []

    def go(copy):
        copy.start()
        sent.append(copy)

    def send_hidden(j):
        part = hidden.at[0, :, pl.ds(pl.multiple_of(shards[j] * block, 128), block)]
        go(remote(part, h_all.at[toks(j)], h_send.at[j - 1], h_recv.at[j - 1], at_shard(shards[j])))

    def hidden_in(j):
        dst = h_all.at[toks(j)]
        remote(dst, dst, h_send.at[j - 1], h_recv.at[j - 1], at_shard(shards[j])).wait_recv()

    def send_upstream(j, h):
        go(remote(
            upstream.at[0, :, cols(h)], u_all.at[toks(j), cols(h)],
            u_send.at[j - 1, h], u_recv.at[j - 1, h], at_shard(shards[j]),
        ))

    def upstream_in(j, h):
        dst = u_all.at[toks(j), cols(h)]
        remote(dst, dst, u_send.at[j - 1, h], u_recv.at[j - 1, h], at_shard(shards[j])).wait_recv()

    def pass_upstream(h):
        upstream_in(2, h)
        go(remote(
            u_all.at[toks(2), cols(h)], u_all.at[toks(3), cols(h)],
            u_send.at[2, h], u_recv.at[2, h], at_shard(sibling),
        ))

    order = tuple(range(1, layers)) + (0,)
    pieces = [(h, d) for h in range(CHUNKS) for d in order]

    def send_piece(h, d):
        part = weights.at[0, row_block(layer(d) * 2 + (1 - x)), cols(h)]
        go(remote(part, x_in.at[d, :, cols(h)], x_send.at[h, d], x_recv.at[h, d], at_rep(x_peer)))

    for piece in pieces[:AHEAD]:
        send_piece(*piece)
    send_hidden(3)
    send_hidden(2)
    for h in range(CHUNKS):
        send_upstream(2, h)
    send_hidden(1)
    for h in range(CHUNKS):
        send_upstream(1, h)

    def project(j, dst):
        @pl.loop(0, columns // 256)
        def _(n):
            at = pl.ds(pl.multiple_of(n * 256, 256), 256)
            dst[:, at] = jnp.dot(h_all[toks(j), :], w[:, at], preferred_element_type=F32)

    def turn(j):
        @pl.loop(0, block // 128)
        def _(i):
            at = pl.ds(pl.multiple_of(i * 128, 128), 128)
            h_t[at, toks(j)] = h_all[toks(j), at].T

    loads[0].wait()
    loads[1].wait()
    project(0, p_own)
    turn(0)
    hidden_in(1)
    project(1, p_out.at[0])
    go(remote(p_out.at[0], p_in.at[0], p_send.at[0], p_recv.at[0], at_shard(sibling)))
    turn(1)

    tall = rows // 3 if rows % 48 == 0 else STRIP

    def pairs(h):
        for d in order:
            dst = x_in.at[d, :, cols(h)]
            remote(dst, dst, x_send.at[h, d], x_recv.at[h, d], at_rep(x_peer)).wait_recv()
            later = h * layers + order.index(d) + AHEAD
            if later < len(pieces):
                send_piece(*pieces[later])
            base = (layer(d) * 2 + x) * rows

            def pair(i, d=d, base=base):
                here = pl.ds(pl.multiple_of(base + i, STRIP), tall)
                total = w[here, cols(h)].astype(F32) + x_in[d, pl.ds(i, tall), cols(h)].astype(F32)
                if d == 0:
                    acc[pl.ds(i, tall), cols(h)] = total
                else:
                    z_out[d - 1, pl.ds(i, tall), cols(h)] = total.astype(BF16)

            strips(rows, pair, tall)
            if d:
                go(remote(
                    z_out.at[d - 1, :, cols(h)], z_in.at[d - 1, :, cols(h)],
                    z_send.at[h, d - 1], z_recv.at[h, d - 1], at_rep(layer(d) * 2 + x),
                ))

    def renew(h):
        for d in range(1, layers):
            dst = z_in.at[d - 1, :, cols(h)]
            remote(dst, dst, z_send.at[h, d - 1], z_recv.at[h, d - 1], at_rep(me_rep)).wait_recv()

        def outer(i):
            here = pl.ds(i, tall)
            summed = acc[here, cols(h)]
            for d in range(1, layers):
                summed = summed + z_in[d - 1, here, cols(h)].astype(F32)
            now = g[here, cols(h)]
            pseudo = now - summed / reps
            momentum = outer_mu * om[here, cols(h)] + pseudo
            renewed = now - outer_rate * (pseudo + outer_mu * momentum)
            mom[here, cols(h)] = momentum
            ren[here, cols(h)] = renewed
            at = pl.ds(pl.multiple_of(me_rep * rows + i, STRIP), tall)
            spread[at, cols(h)] = renewed.astype(BF16)

        strips(rows, outer, tall)
        own = spread.at[row_block(me_rep), cols(h)]
        for d in order[:-1]:
            go(remote(own, own, gz_send.at[h, d - 1], gz_recv.at[h, d - 1], at_rep(layer(d) * 2 + x)))
        go(remote(own, own, gx_send.at[h, 0], gx_recv.at[h, 0], at_rep(x_peer)))

    near_first = (1,) + tuple(range(layers - 1, 1, -1))

    def forward(h):
        for d in near_first:
            part = spread.at[row_block(layer(-d) * 2 + x), cols(h)]
            remote(part, part, gz_send.at[h, d - 1], gz_recv.at[h, d - 1], at_rep(me_rep)).wait_recv()
            go(remote(part, part, gx_send.at[h, d], gx_recv.at[h, d], at_rep(x_peer)))

    part_rows = block // 3
    high = 48 if block % 48 == 0 else STRIP

    def inner(h):
        upstream_in(1, h)
        upstream_in(3, h)

        @pl.loop(0, 3)
        def _(part):
            at = pl.ds(pl.multiple_of(part * part_rows, STRIP), part_rows)
            grad[at, cols(h)] = jnp.dot(h_t[at, :], u_all[:, cols(h)], preferred_element_type=F32)

        def step(i):
            here = (pl.ds(i, high), cols(h))
            grad[here] = half_inner(
                grad[here], m1[here].astype(F32), m2[here].astype(F32), w[here].astype(F32), factor
            )

        strips(block, step, high)

    loads[3].wait()
    loads[4].wait()
    pairs(0)
    pairs(1)
    renew(0)
    pairs(2)
    renew(1)
    pairs(3)
    forward(0)
    renew(2)

    hidden_in(3)
    project(3, p_out.at[1])
    go(remote(p_out.at[1], p_in.at[1], p_send.at[1], p_recv.at[1], at_shard(sibling)))
    turn(3)
    renew(3)
    forward(1)
    hidden_in(2)
    project(2, p_far)
    remote(p_in.at[1], p_in.at[1], p_send.at[1], p_recv.at[1], at_shard(sibling)).wait_recv()

    def chip_sum(i):
        here = pl.ds(i, STRIP)
        y_out[here, :] = (p_far[here, :] + p_in[1, here, :]).astype(BF16)

    strips(tokens, chip_sum)
    go(remote(y_out, y_in, p_send.at[2], p_recv.at[2], at_shard(across)))
    forward(2)
    turn(2)
    loads[2].wait()
    loads[5].wait()
    loads[6].wait()
    pass_upstream(0)
    pass_upstream(1)
    forward(3)
    inner(0)
    pass_upstream(2)
    inner(1)
    pass_upstream(3)
    inner(2)
    inner(3)

    remote(p_in.at[0], p_in.at[0], p_send.at[0], p_recv.at[0], at_shard(sibling)).wait_recv()
    remote(y_in, y_in, p_send.at[2], p_recv.at[2], at_shard(across)).wait_recv()

    def finish(i):
        here = pl.ds(i, STRIP)
        total = p_own[here, :] + p_in[0, here, :] + y_in[here, :].astype(F32)
        val[here, :] = (total * factor).astype(BF16)

    strips(tokens, finish)

    def merge(owner):
        base = owner * rows

        def body(i):
            here = pl.ds(pl.multiple_of(base + i, STRIP), STRIP)
            mer[here, :] = (grad[here, :] + (1.0 - mixing) * spread[here, :].astype(F32)).astype(BF16)

        strips(rows, body)

    merge(me_rep)
    for d in near_first:
        merge(layer(-d) * 2 + x)
    for d in (0,) + near_first:
        owner = layer(-d) * 2 + (1 - x)
        for h in range(CHUNKS):
            part = spread.at[row_block(owner), cols(h)]
            remote(part, part, gx_send.at[h, d], gx_recv.at[h, d], at_rep(x_peer)).wait_recv()
        merge(owner)

    for copy in sent:
        copy.wait_send()


def fused_call(reps, hidden, upstream, weights, moment_one, moment_two, global_params, outer_momentum):
    tokens = hidden.shape[1]
    block, columns = weights.shape[1:]
    rows = block // reps
    layers = reps // 2
    dma = pltpu.SemaphoreType.DMA
    scratch = [
        pltpu.VMEM((4 * tokens, block), BF16),
        pltpu.VMEM((block, 4 * tokens), BF16),
        pltpu.VMEM((4 * tokens, columns), BF16),
        pltpu.VMEM((block, columns), BF16),
        pltpu.VMEM((block, columns), BF16),
        pltpu.VMEM((block, columns), BF16),
        pltpu.VMEM((rows, columns), F32),
        pltpu.VMEM((rows, columns), F32),
        pltpu.VMEM((layers, rows, columns), BF16),
        pltpu.VMEM((layers - 1, rows, columns), BF16),
        pltpu.VMEM((layers - 1, rows, columns), BF16),
        pltpu.VMEM((rows, columns), F32),
        pltpu.VMEM((block, columns), BF16),
        pltpu.VMEM((block, columns), F32),
        pltpu.VMEM((tokens, columns), F32),
        pltpu.VMEM((tokens, columns), F32),
        pltpu.VMEM((2, tokens, columns), F32),
        pltpu.VMEM((2, tokens, columns), F32),
        pltpu.VMEM((tokens, columns), BF16),
        pltpu.VMEM((tokens, columns), BF16),
        dma((7,)),
        dma((3,)), dma((3,)), dma((3, CHUNKS)), dma((3, CHUNKS)), dma((3,)), dma((3,)),
        dma((CHUNKS, layers)), dma((CHUNKS, layers)),
        dma((CHUNKS, layers - 1)), dma((CHUNKS, layers - 1)),
        dma((CHUNKS, layers - 1)), dma((CHUNKS, layers - 1)),
        dma((CHUNKS, layers)), dma((CHUNKS, layers)),
    ]
    anywhere = pl.BlockSpec(memory_space=pl.ANY)
    results = pl.pallas_call(
        functools.partial(fused, reps),
        out_shape=(
            pltpu.VMEM((tokens, columns), BF16),
            pltpu.VMEM((block, columns), BF16),
            pltpu.VMEM((rows, columns), F32),
            pltpu.VMEM((rows, columns), F32),
        ),
        in_specs=[anywhere] * 7,
        out_specs=[pl.BlockSpec(memory_space=pltpu.VMEM)] * 4,
        scratch_shapes=scratch,
        compiler_params=pltpu.CompilerParams(
            collective_id=0, has_side_effects=True, vmem_limit_bytes=59 * 1024 * 1024
        ),
        cost_estimate=pl.CostEstimate(
            flops=4 * tokens * hidden.shape[2] * columns, bytes_accessed=18 * 1024 * 1024, transcendentals=0
        ),
    )(hidden, upstream, weights, moment_one, moment_two, global_params, outer_momentum)
    return pl.pallas_call(
        write_out,
        out_shape=tuple(jax.ShapeDtypeStruct((1,) + a.shape, a.dtype) for a in results),
        in_specs=[pl.BlockSpec(memory_space=pltpu.VMEM)] * 4,
        out_specs=[anywhere] * 4,
        scratch_shapes=[dma((4,))],
        compiler_params=pltpu.CompilerParams(vmem_limit_bytes=8 * 1024 * 1024),
        cost_estimate=pl.CostEstimate(flops=0, bytes_accessed=8 * 1024 * 1024, transcendentals=0),
    )(*results)


def write_out(*refs):
    sources, targets, done = refs[:4], refs[4:8], refs[8]
    copies = [
        pltpu.make_async_copy(a, b.at[0], done.at[i]) for i, (a, b) in enumerate(zip(sources, targets))
    ]
    for copy in copies:
        copy.start()
    for copy in copies:
        copy.wait()


def collective_form(hidden, upstream, weights, moment_one, moment_two, global_params, outer_momentum):
    factor = float(hidden.shape[2]) ** (-0.5)
    tokens, grads_in = hidden[0], upstream[0]
    gathered = lax.all_gather(weights, "fsdp", axis=1, tiled=True)[0]
    values = (jnp.dot(tokens, gathered, preferred_element_type=F32) * factor).astype(BF16)
    partial = lax.dot_general(tokens, grads_in, (((0,), (0,)), ((), ())), preferred_element_type=F32)
    gradient = lax.psum_scatter(
        (partial * factor).astype(BF16), "fsdp", scatter_dimension=0, tiled=True
    ).astype(F32)
    updated = inner_step(
        gradient, moment_one[0].astype(F32), moment_two[0].astype(F32), weights[0].astype(F32)
    )
    owned = lax.psum_scatter(weights.astype(F32), "rep", scatter_dimension=1, tiled=True)
    pseudo = global_params - owned / lax.axis_size("rep")
    momentum = outer_mu * outer_momentum + pseudo
    renewed = global_params - outer_rate * (pseudo + outer_mu * momentum)
    spread = lax.all_gather(renewed.astype(BF16), "rep", axis=1, tiled=True).astype(F32)[0]
    merged = (mixing * updated + (1.0 - mixing) * spread).astype(BF16)
    return (values[None], merged[None], renewed, momentum)


def solution(mesh):
    reps, shards = mesh.shape["rep"], mesh.shape["fsdp"]

    def on_device(*arrays):
        rows = arrays[5].shape[1]
        if shards == 4 and reps % 2 == 0 and reps > 2 and rows % STRIP == 0:
            return fused_call(reps, *arrays)
        return collective_form(*arrays)

    return jax.shard_map(
        on_device,
        mesh=mesh,
        in_specs=(P("rep", "fsdp", None),) * 5 + (P("fsdp", "rep", None),) * 2,
        out_specs=(P("rep", "fsdp", None),) * 2 + (P("fsdp", "rep", None),) * 2,
        check_vma=False,
    )
```
